32 devices in a mesh: row: 8 (over z, y), head: 4 (over x, core).
Axes of the slice: x: 2, y: 2, z: 4, core: 2. Of those that a mesh axis runs over, the one named last changes fastest.
Arguments:
- samples: bfloat16 [16, 512, 2048], P('row', None, 'head'), may hold values from -12 to 12
- norm_gain: float32 [2048], replicated, may hold values from 0.25 to 1.75
- row_qkv: bfloat16 [3, 2048, 1024], P(None, None, 'head'), may hold values from -0.09082975 to 0.09082975
- col_qkv: bfloat16 [3, 2048, 1024], P(None, None, 'head'), may hold values from -0.09082975 to 0.09082975
- row_out: bfloat16 [1024, 2048], P('head'), may hold values from -0.1875 to 0.1875
- col_out: bfloat16 [1024, 2048], P('head'), may hold values from -0.1875 to 0.1875
Outputs:
- layer_out: bfloat16 [16, 512, 2048], P('row', None, 'head')
The draws below stay inside these ranges and needn't reach their ends.
All inputs are finite; a program needn't handle non-finite values.
Results may differ from the reference program's by a relative error of at most 0.012.
Values may be sent and summed in bfloat16 or wider, within the bound.
A program may use at most 64 MiB of HBM per device.

```python
import jax
import jax.numpy as jnp
from jax import lax

D = 2048
HD = 128
RHEADS = 8
CHEADS = 8
COLS = 512
ROWS = 16


def draw_samples(key, part):
    own_key = jax.random.fold_in(key, 3)
    gaussian = jnp.clip(jax.random.normal(own_key, (ROWS, COLS, D), jnp.float32), -6.0, 6.0)
    return gaussian.astype(jnp.bfloat16)


def draw_row_qkv(key, part):
    own_key = jax.random.fold_in(key, 5)
    weights = jnp.clip(jax.random.normal(own_key, (3, D, RHEADS * HD), jnp.float32), -3.98, 3.98) * D ** (-0.5)
    return weights.astype(jnp.bfloat16)


def draw_col_qkv(key, part):
    own_key = jax.random.fold_in(key, 7)
    weights = jnp.clip(jax.random.normal(own_key, (3, D, CHEADS * HD), jnp.float32), -3.98, 3.98) * D ** (-0.5)
    return weights.astype(jnp.bfloat16)


def strengthened(drawn, key, source, target, blocks, factor):
    def block_of(position):
        return (jnp.arange(drawn.shape[position]) // (drawn.shape[position] // blocks)).reshape((-1,) + (1,) * (drawn.ndim - 1 - position))

    one_side = jax.random.permutation(key, blocks)[block_of(target)]
    other_side = (block_of(target) + blocks // 2) % blocks
    return jnp.where((block_of(source) == one_side) | (block_of(source) == other_side), factor * drawn, drawn)


def block_scale(stream_key, extent, shards, smallest, top_value):
    loudness = 1.0
    for dim, shards_of in shards:
        heights = jax.random.uniform(jax.random.fold_in(jax.random.fold_in(stream_key, 6), dim), (shards_of,), jnp.float32, smallest / len(shards), top_value / len(shards))
        loudness = loudness * jnp.repeat(jnp.exp(heights), extent[dim] // shards_of).reshape((-1,) + (1,) * (len(extent) - 1 - dim))
    return loudness


def bell_draw_with(stream_key, shape, deviation, bound, split, heavy, kind=jnp.bfloat16):
    drawn = deviation * jax.random.normal(stream_key, shape, jnp.float32)
    if split:
        drawn = drawn * block_scale(stream_key, shape, split, -0.22, 0.18)
    return jnp.clip(strengthened(drawn, jax.random.fold_in(stream_key, 3), *heavy), -bound, bound).astype(kind)


def setup_inputs(seed: int = 0) -> dict:
    arg_keys = jax.random.split(jax.random.key(seed), 7)
    samples = draw_samples(jax.random.fold_in(arg_keys[6], 71), 0)
    norm_gain = jnp.clip(1.0 + 0.15 * jax.random.normal(arg_keys[1], (D,), jnp.float32), 0.25, 1.75)
    row_qkv = draw_row_qkv(jax.random.fold_in(arg_keys[6], 71), 0)
    col_qkv = draw_col_qkv(jax.random.fold_in(arg_keys[6], 71), 0)
    row_out = bell_draw_with(arg_keys[4], (RHEADS * HD, D), ((RHEADS + CHEADS) * HD) ** -0.5, 0.1875, ((0, 4),), (0, 1, 4, 2.0))
    col_out = bell_draw_with(arg_keys[5], (CHEADS * HD, D), ((RHEADS + CHEADS) * HD) ** -0.5, 0.1875, ((0, 4),), (0, 1, 4, 2.0))
    return {"samples": samples, "norm_gain": norm_gain, "row_qkv": row_qkv, "col_qkv": col_qkv, "row_out": row_out, "col_out": col_out}


def layer_norm(values, norm_gain):
    values = values.astype(jnp.float32)
    mean = lax.optimization_barrier(jnp.mean(values, axis=-1, keepdims=True))
    centred = values - mean
    var = lax.optimization_barrier(jnp.mean(centred * centred, axis=-1, keepdims=True))
    return (centred * lax.rsqrt(var + 1e-05) * norm_gain).astype(jnp.bfloat16)

def softmax_rounded(scores, allowed):
    scores = jnp.where(allowed, scores, -jnp.inf)
    top = lax.optimization_barrier(jnp.max(scores, axis=-1, keepdims=True))
    expo = jnp.exp(scores - top)
    return (expo / lax.optimization_barrier(jnp.sum(expo, axis=-1, keepdims=True))).astype(jnp.bfloat16)

def reference(samples, norm_gain, row_qkv, col_qkv, row_out, col_out):
    scale = 1.0 / HD ** 0.5
    normed = layer_norm(samples, norm_gain).reshape(ROWS * COLS, D)
    row_parts = [jnp.dot(normed, row_qkv[t], preferred_element_type=jnp.float32).astype(jnp.bfloat16) for t in range(3)]
    col_parts = [jnp.dot(normed, col_qkv[t], preferred_element_type=jnp.float32).astype(jnp.bfloat16) for t in range(3)]
    row_stack = jnp.stack(row_parts).reshape(3, ROWS, COLS, RHEADS, HD)
    col_stack = jnp.stack(col_parts).reshape(3, ROWS, COLS, CHEADS, HD)
    causal_cols = jnp.arange(COLS)[:, None] >= jnp.arange(COLS)[None, :]

    def one_row(parts):
        query, keys, vals = (parts[0].astype(jnp.float32), parts[1].astype(jnp.float32), parts[2].astype(jnp.float32))
        scores = jnp.einsum('qhe,khe->hqk', query, keys) * scale
        weights = softmax_rounded(scores, causal_cols[None])
        return jnp.einsum('hqk,khe->qhe', weights.astype(jnp.float32), vals).astype(jnp.bfloat16)
    row_attn = lax.map(one_row, jnp.transpose(row_stack, (1, 0, 2, 3, 4)))
    causal_rows = jnp.arange(ROWS)[:, None] >= jnp.arange(ROWS)[None, :]

    def one_head(parts):
        query, keys, vals = (parts[0].astype(jnp.float32), parts[1].astype(jnp.float32), parts[2].astype(jnp.float32))
        scores = jnp.einsum('qce,kce->cqk', query, keys) * scale
        weights = softmax_rounded(scores, causal_rows[None])
        return jnp.einsum('cqk,kce->qce', weights.astype(jnp.float32), vals).astype(jnp.bfloat16)
    col_attn = lax.map(one_head, jnp.transpose(col_stack, (3, 0, 1, 2, 4)))
    col_attn = jnp.transpose(col_attn, (1, 2, 0, 3))
    projected = jnp.dot(row_attn.reshape(ROWS * COLS, RHEADS * HD), row_out, preferred_element_type=jnp.float32)
    projected = projected + jnp.dot(col_attn.reshape(ROWS * COLS, CHEADS * HD), col_out, preferred_element_type=jnp.float32)
    total = samples.astype(jnp.float32) + projected.reshape(ROWS, COLS, D)
    return total.astype(jnp.bfloat16)
```

```python
import functools

import jax
import jax.numpy as jnp
from jax import lax
from jax.experimental import pallas as pl
from jax.experimental.pallas import tpu as pltpu
from jax.sharding import PartitionSpec as P

HD = 128
MESH = pl.DeviceIdType.MESH
F32 = jnp.float32
BF16 = jnp.bfloat16


def attend(query, keys, vals, allowed):
    scores = lax.dot_general(query, keys, (((1,), (1,)), ((), ())), preferred_element_type=F32)
    scores = jnp.where(allowed, scores * (1.0 / HD**0.5), -jnp.inf)
    expo = jnp.exp(scores - jnp.max(scores, axis=-1, keepdims=True))
    total = jnp.sum(expo, axis=-1, keepdims=True)
    out = jnp.dot(expo.astype(BF16), vals, preferred_element_type=F32)
    return (out / total).astype(BF16)


def layer_kernel(
    n, chunks,
    samples, gain, row_qkv, col_qkv, row_out, col_out, out,
    gathered, wqkv, wout, normed, row_store, col_send, col_recv, col_done, col_back, row_attn,
    part_send, part_recv, kept, cross_send, cross_recv, result,
    load_sem, own_sem, store_sem, x_sem, core_sem, fwd_sem, col_sem, back_sem, part_sem, cross_sem,
):
    rows, cols, feat = samples.shape
    width = cols // chunks
    tokens = rows * width
    each = width // n
    local = row_qkv.shape[2]
    heads = local // HD
    me = lax.axis_index("row")
    head = lax.axis_index("head")
    x_own = head // 2
    core = head % 2
    x_other = 1 - x_own
    core_other = 1 - core
    x_peer = x_other * 2 + core
    core_peer = x_own * 2 + core_other

    def chunk(k):
        return pl.ds(k * width, width)

    loads = [
        pltpu.make_async_copy(row_qkv, wqkv.at[pl.ds(0, 3)], load_sem.at[0]),
        pltpu.make_async_copy(col_qkv, wqkv.at[pl.ds(3, 3)], load_sem.at[1]),
    ]
    own = [
        pltpu.make_async_copy(samples.at[:, chunk(k)], gathered.at[k, head], own_sem.at[k])
        for k in range(chunks)
    ]
    out_loads = []
    for j in range(4):
        for i, ref in enumerate((row_out, col_out)):
            out_loads.append(
                pltpu.make_async_copy(
                    ref.at[:, pl.ds(j * feat, feat)],
                    wout.at[j, pl.ds(i * local, local)],
                    load_sem.at[2 + j * 2 + i],
                )
            )
    own[0].start()
    for copy in loads + own[1:] + out_loads:
        copy.start()

    barrier = pltpu.get_barrier_semaphore()
    pl.semaphore_signal(barrier, inc=1, device_id={"head": x_peer}, device_id_type=MESH)
    pl.semaphore_signal(barrier, inc=1, device_id={"head": core_peer}, device_id_type=MESH)
    for d in range(1, n):
        pl.semaphore_signal(barrier, inc=1, device_id={"row": lax.rem(me + d, n)}, device_id_type=MESH)
    pl.semaphore_wait(barrier, n + 1)

    def remote(src, dst, sems, where, peer):
        return pltpu.make_async_remote_copy(
            src_ref=src, dst_ref=dst, send_sem=sems.at[(0,) + where], recv_sem=sems.at[(1,) + where],
            device_id=peer, device_id_type=MESH,
        )

    x_copies = [
        remote(samples.at[:, chunk(k)], gathered.at[k, head], x_sem, (k,), {"head": x_peer})
        for k in range(chunks)
    ]
    core_copies = [
        remote(samples.at[:, chunk(k)], gathered.at[k, head], core_sem, (k,), {"head": core_peer})
        for k in range(chunks)
    ]
    fwd_copies = [
        remote(gathered.at[k, x_peer], gathered.at[k, x_peer], fwd_sem, (k,), {"head": core_peer})
        for k in range(chunks)
    ]
    col_copies, back_copies, part_copies, cross_copies, stores = {}, {}, {}, {}, {}

    def send_samples(k):
        if k < chunks:
            x_copies[k].start()
            core_copies[k].start()

    def pass_on(k):
        x_copies[k].wait_recv()
        fwd_copies[k].start()
        send_samples(k + 2)

    def project(k):
        own[k].wait()
        core_copies[k].wait_recv()
        fwd_copies[k].wait_recv()
        step = 16
        for r in range(rows):

            @pl.loop(0, width // step)
            def _(i):
                at = pl.ds(pl.multiple_of(i * step, step), step)
                vals = [gathered[k, j, r, at, :].astype(F32) for j in range(4)]
                mean = sum(jnp.sum(v, axis=-1, keepdims=True) for v in vals) * (1.0 / (4 * feat))
                vals = [v - mean for v in vals]
                var = sum(jnp.sum(v * v, axis=-1, keepdims=True) for v in vals) * (1.0 / (4 * feat))
                inv = lax.rsqrt(var + 1e-05)
                to = pl.ds(pl.multiple_of(r * width + i * step, step), step)
                for j in range(4):
                    g = gain[:, j * feat:(j + 1) * feat]
                    normed[to, j * feat:(j + 1) * feat] = (vals[j] * inv * g).astype(BF16)

        if k == 0:
            for copy in loads:
                copy.wait()

        def mixed(t):
            value = jnp.dot(normed[...], wqkv[t], preferred_element_type=F32)
            return value.astype(BF16).reshape(rows, width, local)

        @pl.loop(0, 3)
        def _(t):
            col_send[k, t] = mixed(t + 3)

        for d in range(1, n):
            peer = lax.rem(me + d, n)
            cut = pl.ds(pl.multiple_of(peer * each, each), each)
            col_copies[k, d] = remote(
                col_send.at[k, :, :, cut], col_recv.at[k, me], col_sem, (k, d), {"row": peer}
            )
            col_copies[k, d].start()
        mine = pl.ds(pl.multiple_of(me * each, each), each)
        col_recv[k, me] = col_send[k, :, :, mine, :]

        @pl.loop(0, 3)
        def _(t):
            row_store[t, :, chunk(k), :] = mixed(t)

    def row_attend(k):
        seen = (k + 1) * width
        i = lax.broadcasted_iota(jnp.int32, (width, seen), 0) + k * width
        j = lax.broadcasted_iota(jnp.int32, (width, seen), 1)
        for r in range(rows):
            for h in range(heads):
                lanes = pl.ds(h * HD, HD)
                row_attn[k, r, :, lanes] = attend(
                    row_store[0, r, chunk(k), lanes],
                    row_store[1, r, pl.ds(0, seen), lanes],
                    row_store[2, r, pl.ds(0, seen), lanes],
                    j <= i,
                )

    def col_attend(k):
        for d in range(1, n):
            col_copies[k, d].wait_recv()
        held = n * rows * each
        i = lax.broadcasted_iota(jnp.int32, (held, held), 0)
        j = lax.broadcasted_iota(jnp.int32, (held, held), 1)
        allowed = (j <= i) & (lax.rem(i, each) == lax.rem(j, each))
        for h in range(heads):
            lanes = pl.ds(h * HD, HD)
            parts = [col_recv[k, :, t, :, :, lanes].reshape(held, HD) for t in range(3)]
            col_done[k, :, :, :, lanes] = attend(*parts, allowed).reshape(n, rows, each, HD)
        mine = pl.ds(pl.multiple_of(me * each, each), each)
        for d in range(1, n):
            peer = lax.rem(me + d, n)
            back_copies[k, d] = remote(
                col_done.at[k, peer], col_back.at[k, :, mine], back_sem, (k, d), {"row": peer}
            )
            back_copies[k, d].start()
        col_back[k, :, mine, :] = col_done[k, me]

    def finish(k):
        if k == 0:
            for copy in out_loads:
                copy.wait()
        for d in range(1, n):
            back_copies[k, d].wait_recv()
        attn = jnp.concatenate(
            [row_attn[k].reshape(tokens, local), col_back[k].reshape(tokens, local)], axis=-1
        )

        def block(j):
            return jnp.dot(attn, wout[j], preferred_element_type=F32)

        for s, xb in enumerate((x_other, x_own)):
            part_send[k, s] = block(xb * 2 + core_other).astype(BF16).reshape(rows, width, feat)
            part_copies[k, s] = remote(
                part_send.at[k, s], part_recv.at[k, s], part_sem, (k, s), {"head": core_peer}
            )
            part_copies[k, s].start()
        for s, xb in enumerate((x_other, x_own)):
            kept[k, s] = block(xb * 2 + core).reshape(rows, width, feat)

    def cross(k):
        part_copies[k, 0].wait_recv()
        cross_send[k] = (kept[k, 0] + part_recv[k, 0].astype(F32)).astype(BF16)
        cross_copies[k] = remote(
            cross_send.at[k], cross_recv.at[k], cross_sem, (k,), {"head": x_peer}
        )
        cross_copies[k].start()

    def close(k):
        part_copies[k, 1].wait_recv()
        cross_copies[k].wait_recv()
        total = kept[k, 1] + part_recv[k, 1].astype(F32) + cross_recv[k].astype(F32)
        result[k] = (gathered[k, head].astype(F32) + total).astype(BF16)
        stores[k] = pltpu.make_async_copy(result.at[k], out.at[:, chunk(k)], store_sem.at[k])
        stores[k].start()

    send_samples(0)
    send_samples(1)
    pass_on(0)
    project(0)
    pass_on(1)
    row_attend(0)
    project(1)
    pass_on(2)
    row_attend(1)
    project(2)
    col_attend(0)
    pass_on(3)
    row_attend(2)
    project(3)
    row_attend(3)
    col_attend(1)
    finish(0)
    cross(0)
    col_attend(2)
    finish(1)
    cross(1)
    close(0)
    col_attend(3)
    finish(2)
    cross(2)
    close(1)
    finish(3)
    cross(3)
    close(2)
    close(3)

    for group in (x_copies, core_copies, fwd_copies):
        for copy in group:
            copy.wait_send()
    for group in (col_copies, back_copies, part_copies, cross_copies):
        for copy in group.values():
            copy.wait_send()
    for copy in stores.values():
        copy.wait()


def fused(n, samples, norm_gain, row_qkv, col_qkv, row_out, col_out):
    rows, cols, feat = samples.shape
    chunks = 4
    width = cols // chunks
    each = width // n
    local = row_qkv.shape[2]
    dma = pltpu.SemaphoreType.DMA
    anywhere = pl.BlockSpec(memory_space=pl.ANY)
    return pl.pallas_call(
        functools.partial(layer_kernel, n, chunks),
        out_shape=jax.ShapeDtypeStruct(samples.shape, samples.dtype),
        in_specs=[anywhere, pl.BlockSpec(memory_space=pltpu.VMEM)] + [anywhere] * 4,
        out_specs=anywhere,
        scratch_shapes=[
            pltpu.VMEM((chunks, 4, rows, width, feat), BF16),
            pltpu.VMEM((6, 4 * feat, local), BF16),
            pltpu.VMEM((4, 2 * local, feat), BF16),
            pltpu.VMEM((rows * width, 4 * feat), BF16),
            pltpu.VMEM((3, rows, cols, local), BF16),
            pltpu.VMEM((chunks, 3, rows, width, local), BF16),
            pltpu.VMEM((chunks, n, 3, rows, each, local), BF16),
            pltpu.VMEM((chunks, n, rows, each, local), BF16),
            pltpu.VMEM((chunks, rows, width, local), BF16),
            pltpu.VMEM((chunks, rows, width, local), BF16),
            pltpu.VMEM((chunks, 2, rows, width, feat), BF16),
            pltpu.VMEM((chunks, 2, rows, width, feat), BF16),
            pltpu.VMEM((chunks, 2, rows, width, feat), F32),
            pltpu.VMEM((chunks, rows, width, feat), BF16),
            pltpu.VMEM((chunks, rows, width, feat), BF16),
            pltpu.VMEM((chunks, rows, width, feat), BF16),
            dma((10,)),
            dma((chunks,)),
            dma((chunks,)),
            dma((2, chunks)),
            dma((2, chunks)),
            dma((2, chunks)),
            dma((2, chunks, n)),
            dma((2, chunks, n)),
            dma((2, chunks, 2)),
            dma((2, chunks)),
        ],
        compiler_params=pltpu.CompilerParams(
            collective_id=0, has_side_effects=True, vmem_limit_bytes=52 * 2**20
        ),
        cost_estimate=pl.CostEstimate(flops=9 * 10**9, bytes_accessed=11 * 2**20, transcendentals=10**6),
    )(samples, norm_gain.reshape(1, -1), row_qkv, col_qkv, row_out, col_out)


def layer_norm(values, norm_gain):
    values = values.astype(F32)
    mean = jnp.mean(values, axis=-1, keepdims=True)
    centred = values - mean
    var = jnp.mean(centred * centred, axis=-1, keepdims=True)
    return (centred * lax.rsqrt(var + 1e-05) * norm_gain).astype(BF16)


def softmax_rounded(scores, allowed):
    scores = jnp.where(allowed, scores, -jnp.inf)
    top = jnp.max(scores, axis=-1, keepdims=True)
    expo = jnp.exp(scores - top)
    return (expo / jnp.sum(expo, axis=-1, keepdims=True)).astype(BF16)


def column_attend(query, keys, vals):
    full_rows = query.shape[0]
    scores = jnp.einsum("qche,kche->chqk", query, keys, preferred_element_type=F32) * (1.0 / HD**0.5)
    allowed = jnp.arange(full_rows)[:, None] >= jnp.arange(full_rows)[None, :]
    weights = softmax_rounded(scores, allowed[None, None])
    return jnp.einsum("chqk,kche->qche", weights, vals, preferred_element_type=F32).astype(BF16)


def unfused(samples, norm_gain, row_qkv, col_qkv, row_out, col_out):
    rows_local, cols, feat_local = samples.shape
    tokens_local = rows_local * cols
    whole = lax.all_gather(samples, "head", axis=2, tiled=True)
    normed = layer_norm(whole, norm_gain).reshape(tokens_local, -1)

    def project(weights):
        mixed = jnp.einsum("nd,tde->tne", normed, weights, preferred_element_type=F32)
        return mixed.astype(BF16).reshape(3, rows_local, cols, -1, HD)

    stacked = project(row_qkv)
    scores = jnp.einsum("rqhe,rkhe->rhqk", stacked[0], stacked[1], preferred_element_type=F32)
    allowed = jnp.arange(cols)[:, None] >= jnp.arange(cols)[None, :]
    weights = softmax_rounded(scores * (1.0 / HD**0.5), allowed[None, None])
    attended = jnp.einsum("rhqk,rkhe->rqhe", weights, stacked[2], preferred_element_type=F32)
    row_attn = attended.astype(BF16).reshape(tokens_local, -1)
    moved = column_attend(
        *(lax.all_to_all(part, "row", split_axis=1, concat_axis=0, tiled=True) for part in project(col_qkv))
    )
    returned = lax.all_to_all(moved, "row", split_axis=0, concat_axis=1, tiled=True)
    partial_term = jnp.dot(row_attn, row_out, preferred_element_type=F32)
    partial_term = partial_term + jnp.dot(
        returned.reshape(tokens_local, -1), col_out, preferred_element_type=F32
    )
    summed = lax.psum_scatter(partial_term.astype(BF16), "head", scatter_dimension=1, tiled=True)
    total = samples.astype(F32) + summed.astype(F32).reshape(rows_local, cols, feat_local)
    return total.astype(BF16)


def solution(mesh):
    n = mesh.shape["row"]

    def shards(samples, *rest):
        if mesh.shape["head"] == 4 and samples.shape[1] % (4 * 16 * n) == 0:
            return fused(n, samples, *rest)
        return unfused(samples, *rest)

    placed = (
        P("row", None, "head"),
        P(),
        P(None, None, "head"),
        P(None, None, "head"),
        P("head", None),
        P("head", None),
    )
    return jax.shard_map(
        shards, mesh=mesh, in_specs=placed, out_specs=P("row", None, "head"), check_vma=False
    )
```

```python
import functools

import jax
import jax.numpy as jnp
from jax import lax
from jax.experimental import pallas as pl
from jax.experimental.pallas import tpu as pltpu
from jax.sharding import PartitionSpec as P

HD = 128
MESH = pl.DeviceIdType.MESH
F32 = jnp.float32
BF16 = jnp.bfloat16


def attend(query, keys, vals, allowed):
    scores = lax.dot_general(query, keys, (((1,), (1,)), ((), ())), preferred_element_type=F32)
    scores = jnp.where(allowed, scores * (1.0 / HD**0.5), -jnp.inf)
    expo = jnp.exp(scores - jnp.max(scores, axis=-1, keepdims=True))
    total = jnp.sum(expo, axis=-1, keepdims=True)
    out = jnp.dot(expo.astype(BF16), vals, preferred_element_type=F32)
    return (out / total).astype(BF16)


def partial_attend(query, keys, vals, allowed):
    scores = lax.dot_general(query, keys, (((1,), (1,)), ((), ())), preferred_element_type=F32)
    scores = jnp.where(allowed, scores * (1.0 / HD**0.5), -jnp.inf)
    top = jnp.max(scores, axis=-1, keepdims=True)
    expo = jnp.exp(scores - top)
    total = jnp.sum(expo, axis=-1, keepdims=True)
    out = jnp.dot(expo.astype(BF16), vals, preferred_element_type=F32)
    return out / total, top + jnp.log(total)


def merge(parts):
    top = functools.reduce(jnp.maximum, [lse for _, lse in parts])
    weights = [jnp.exp(lse - top) for _, lse in parts]
    return sum(w * out for w, (out, _) in zip(weights, parts)) / sum(weights)


def layer_kernel(
    n, chunks,
    samples, gain, row_qkv, col_qkv, row_out, col_out, out,
    gathered, wqkv, wout, normed, row_store, col_send, col_own, col_keys, col_query,
    far_out, far_lse, near_out, near_lse, col_done, col_back, row_attn,
    part_send, part_recv, kept, cross_send, cross_recv, result,
    load_sem, own_sem, store_sem, x_sem, core_sem, fwd_sem, col_sem, far_sem, back_sem, part_sem, cross_sem,
):
    rows, cols, feat = samples.shape
    width = cols // chunks
    tokens = rows * width
    half = width // 2
    local = row_qkv.shape[2]
    heads = local // HD
    me = lax.axis_index("row")
    z = me // 2
    y = me % 2
    y_other = 1 - y
    y_peer = {"row": z * 2 + y_other}
    head = lax.axis_index("head")
    x_own = head // 2
    core = head % 2
    x_other = 1 - x_own
    core_other = 1 - core
    x_peer = x_other * 2 + core
    core_peer = x_own * 2 + core_other

    def chunk(k):
        return pl.ds(k * width, width)

    loads = [
        pltpu.make_async_copy(row_qkv, wqkv.at[pl.ds(0, 3)], load_sem.at[0]),
        pltpu.make_async_copy(col_qkv, wqkv.at[pl.ds(3, 3)], load_sem.at[1]),
    ]
    own = [
        pltpu.make_async_copy(samples.at[:, chunk(k)], gathered.at[k, head], own_sem.at[k])
        for k in range(chunks)
    ]
    out_loads = []
    for j in range(4):
        for i, ref in enumerate((row_out, col_out)):
            out_loads.append(
                pltpu.make_async_copy(
                    ref.at[:, pl.ds(j * feat, feat)],
                    wout.at[j, pl.ds(i * local, local)],
                    load_sem.at[2 + j * 2 + i],
                )
            )
    own[0].start()
    for copy in loads + own[1:] + out_loads:
        copy.start()

    barrier = pltpu.get_barrier_semaphore()
    pl.semaphore_signal(barrier, inc=1, device_id={"head": x_peer}, device_id_type=MESH)
    pl.semaphore_signal(barrier, inc=1, device_id={"head": core_peer}, device_id_type=MESH)
    for d in range(1, n):
        pl.semaphore_signal(barrier, inc=1, device_id={"row": lax.rem(me + d, n)}, device_id_type=MESH)
    pl.semaphore_wait(barrier, n + 1)

    def remote(src, dst, sems, where, peer):
        return pltpu.make_async_remote_copy(
            src_ref=src, dst_ref=dst, send_sem=sems.at[(0,) + where], recv_sem=sems.at[(1,) + where],
            device_id=peer, device_id_type=MESH,
        )

    x_copies = [
        remote(samples.at[:, chunk(k)], gathered.at[k, head], x_sem, (k,), {"head": x_peer})
        for k in range(chunks)
    ]
    core_copies = [
        remote(samples.at[:, chunk(k)], gathered.at[k, head], core_sem, (k,), {"head": core_peer})
        for k in range(chunks)
    ]
    fwd_copies = [
        remote(gathered.at[k, x_peer], gathered.at[k, x_peer], fwd_sem, (k,), {"head": core_peer})
        for k in range(chunks)
    ]
    part_copies, cross_copies, stores = {}, {}, {}

    def send_samples(k):
        if k < chunks:
            x_copies[k].start()
            core_copies[k].start()

    def pass_on(k):
        x_copies[k].wait_recv()
        fwd_copies[k].start()
        send_samples(k + 2)

    def project(k):
        own[k].wait()
        core_copies[k].wait_recv()
        fwd_copies[k].wait_recv()
        step = 16
        for r in range(rows):

            @pl.loop(0, width // step)
            def _(i):
                at = pl.ds(pl.multiple_of(i * step, step), step)
                vals = [gathered[k, j, r, at, :].astype(F32) for j in range(4)]
                mean = sum(jnp.sum(v, axis=-1, keepdims=True) for v in vals) * (1.0 / (4 * feat))
                vals = [v - mean for v in vals]
                var = sum(jnp.sum(v * v, axis=-1, keepdims=True) for v in vals) * (1.0 / (4 * feat))
                inv = lax.rsqrt(var + 1e-05)
                to = pl.ds(pl.multiple_of(r * width + i * step, step), step)
                for j in range(4):
                    g = gain[:, j * feat:(j + 1) * feat]
                    normed[to, j * feat:(j + 1) * feat] = (vals[j] * inv * g).astype(BF16)

        if k == 0:
            for copy in loads:
                copy.wait()

        def mixed(t):
            value = jnp.dot(normed[...], wqkv[t], preferred_element_type=F32)
            return value.astype(BF16).reshape(rows, width, local)

        @pl.loop(0, 3)
        def _(t):
            col_send[k, t] = mixed(t + 3)

        send_columns(k)

        @pl.loop(0, 3)
        def _(t):
            row_store[t, :, chunk(k), :] = mixed(t)

    def row_attend(k):
        seen = (k + 1) * width
        i = lax.broadcasted_iota(jnp.int32, (width, seen), 0) + k * width
        j = lax.broadcasted_iota(jnp.int32, (width, seen), 1)
        for r in range(rows):
            for h in range(heads):
                lanes = pl.ds(h * HD, HD)
                row_attn[k, r, :, lanes] = attend(
                    row_store[0, r, chunk(k), lanes],
                    row_store[1, r, pl.ds(0, seen), lanes],
                    row_store[2, r, pl.ds(0, seen), lanes],
                    j <= i,
                )

    mine = pl.ds(pl.multiple_of(y * half, half), half)
    theirs = pl.ds(pl.multiple_of(y_other * half, half), half)
    own_rows = pl.ds(y * rows, rows)

    def column_copy(src, dst, k, sent, received, peer):
        return pltpu.make_async_remote_copy(
            src_ref=src, dst_ref=dst, send_sem=col_sem.at[0, k, sent], recv_sem=col_sem.at[1, k, received],
            device_id=peer, device_id_type=MESH,
        )

    def to_peer(k):
        return column_copy(
            col_send.at[k, :, :, theirs], col_own.at[k, :, own_rows], k, 0, 0, y_peer
        )

    def keys_copy(k, to):
        return column_copy(
            col_send.at[k, pl.ds(1, 2), :, pl.ds(to * half, half)], col_keys.at[k, :, own_rows],
            k, 1 + to, 1 + y, {"row": 2 + to},
        )

    def query_copy(k, slot, sent, to_z, to):
        return column_copy(
            col_send.at[k, 0, :, pl.ds(to * half, half)], col_query.at[k, slot, own_rows],
            k, sent + to, 3 + 2 * slot + y, {"row": to_z * 2 + to},
        )

    def column_sends(k, act):
        act(to_peer(k))

        @pl.when(z == 0)
        def _():
            for to in range(2):
                act(keys_copy(k, to))

        @pl.when(z == 2)
        def _():
            for to in range(2):
                act(query_copy(k, 0, 3, 1, to))

        @pl.when(z == 3)
        def _():
            for to in range(2):
                act(query_copy(k, 1, 5, 1, to))
                act(query_copy(k, 0, 3, 2, to))

    def send_columns(k):
        column_sends(k, lambda copy: copy.start())
        col_own[k, :, own_rows] = col_send[k, :, :, mine, :]

    def keys_arrive(k):
        for src in range(2):
            column_copy(
                col_keys.at[k, :, pl.ds(src * rows, rows)], col_keys.at[k, :, pl.ds(src * rows, rows)],
                k, 1 + src, 1 + src, y_peer,
            ).wait_recv()

    def query_arrives(k, slot):
        for src in range(2):
            where = col_query.at[k, slot, pl.ds(src * rows, rows)]
            column_copy(where, where, k, 3 + 2 * slot + src, 3 + 2 * slot + src, y_peer).wait_recv()

    def far_copies(k, slot, to_slot, to_z):
        return [
            pltpu.make_async_remote_copy(
                src_ref=src.at[k, slot], dst_ref=dst.at[k, to_slot],
                send_sem=far_sem.at[0, k, slot, i], recv_sem=far_sem.at[1, k, to_slot, i],
                device_id={"row": to_z * 2 + y}, device_id_type=MESH,
            )
            for i, (src, dst) in enumerate(((far_out, near_out), (far_lse, near_lse)))
        ]

    def far_sends(k, act):
        @pl.when(z == 1)
        def _():
            for copy in far_copies(k, 0, 0, 2) + far_copies(k, 1, 0, 3):
                act(copy)

        @pl.when(z == 2)
        def _():
            for copy in far_copies(k, 0, 1, 3):
                act(copy)

    band = 32
    held = 2 * rows * band

    def block_of(ref, where, cut, lanes):
        return ref[where + (slice(None), cut, lanes)].reshape(held, HD)

    def mask(blocks, causal):
        i = lax.broadcasted_iota(jnp.int32, (held, blocks * held), 0)
        j = lax.broadcasted_iota(jnp.int32, (held, blocks * held), 1)
        same = lax.rem(i, band) == lax.rem(j, band)
        return same & (j <= i + (blocks - 1) * held) if causal else same

    def pieces():
        for b in range(half // band):
            for h in range(heads):
                yield b, h, pl.ds(b * band, band), pl.ds(h * HD, HD)

    def keys_of(k, cut, lanes, both):
        found = []
        for t in (1, 2):
            own_part = block_of(col_own, (k, t), cut, lanes)
            if both:
                own_part = jnp.concatenate([block_of(col_keys, (k, t - 1), cut, lanes), own_part], axis=0)
            found.append(own_part)
        return found

    def far_attend(k, slot, both):
        lane = lax.broadcasted_iota(jnp.int32, (held, HD), 1)
        allowed = mask(2 if both else 1, False)
        stats = {}
        for b, h, cut, lanes in pieces():
            value, lse = partial_attend(
                block_of(col_query, (k, slot), cut, lanes), *keys_of(k, cut, lanes, both), allowed
            )
            far_out[k, slot, :, cut, lanes] = value.astype(BF16).reshape(2 * rows, band, HD)
            stats[b] = jnp.where(lane == h, lse, stats.get(b, jnp.zeros((held, HD), F32)))
        for b, stat in stats.items():
            far_lse[k, slot, b] = jnp.transpose(stat)[:8]

    def col_visit(k):
        to_peer(k).wait_recv()

        @pl.when(z == 1)
        def _():
            keys_arrive(k)
            for slot in range(2):
                query_arrives(k, slot)
                far_attend(k, slot, True)
                for copy in far_copies(k, slot, 0, 2 + slot):
                    copy.start()

        @pl.when(z == 2)
        def _():
            query_arrives(k, 0)
            far_attend(k, 0, False)
            for copy in far_copies(k, 0, 1, 3):
                copy.start()

    def back_copy(k):
        return remote(
            col_done.at[k, pl.ds(y_other * rows, rows)], col_back.at[k, :, mine], back_sem, (k,), y_peer
        )

    def own_attend(k, both, slots):
        for slot in range(slots):
            for copy in far_copies(k, slot, slot, 0):
                copy.wait_recv()
        allowed = mask(2 if both else 1, True)
        stats = {}
        for b, h, cut, lanes in pieces():
            parts = [
                partial_attend(
                    block_of(col_own, (k, 0), cut, lanes), *keys_of(k, cut, lanes, both), allowed
                )
            ]
            for slot in range(slots):
                if (slot, b) not in stats:
                    stats[slot, b] = jnp.transpose(jnp.concatenate([near_lse[k, slot, b]] * (HD // 8), axis=0))
                parts.append(
                    (block_of(near_out, (k, slot), cut, lanes).astype(F32), stats[slot, b][:, h:h + 1])
                )
            value = merge(parts) if slots else parts[0][0]
            col_done[k, :, cut, lanes] = value.astype(BF16).reshape(2 * rows, band, HD)

    def col_attend(k):
        for at, (both, slots) in enumerate(((False, 0), (True, 0), (False, 1), (False, 2))):

            @pl.when(z == at)
            def _(both=both, slots=slots):
                own_attend(k, both, slots)

        back_copy(k).start()
        col_back[k, :, mine, :] = col_done[k, own_rows]

    def finish(k):
        if k == 0:
            for copy in out_loads:
                copy.wait()
        back_copy(k).wait_recv()
        attn = jnp.concatenate(
            [row_attn[k].reshape(tokens, local), col_back[k].reshape(tokens, local)], axis=-1
        )

        def block(j):
            return jnp.dot(attn, wout[j], preferred_element_type=F32)

        for s, xb in enumerate((x_other, x_own)):
            part_send[k, s] = block(xb * 2 + core_other).astype(BF16).reshape(rows, width, feat)
            part_copies[k, s] = remote(
                part_send.at[k, s], part_recv.at[k, s], part_sem, (k, s), {"head": core_peer}
            )
            part_copies[k, s].start()
        for s, xb in enumerate((x_other, x_own)):
            kept[k, s] = block(xb * 2 + core).reshape(rows, width, feat)

    def cross(k):
        part_copies[k, 0].wait_recv()
        cross_send[k] = (kept[k, 0] + part_recv[k, 0].astype(F32)).astype(BF16)
        cross_copies[k] = remote(
            cross_send.at[k], cross_recv.at[k], cross_sem, (k,), {"head": x_peer}
        )
        cross_copies[k].start()

    def close(k):
        part_copies[k, 1].wait_recv()
        cross_copies[k].wait_recv()
        total = kept[k, 1] + part_recv[k, 1].astype(F32) + cross_recv[k].astype(F32)
        result[k] = (gathered[k, head].astype(F32) + total).astype(BF16)
        stores[k] = pltpu.make_async_copy(result.at[k], out.at[:, chunk(k)], store_sem.at[k])
        stores[k].start()

    send_samples(0)
    send_samples(1)
    pass_on(0)
    project(0)
    pass_on(1)
    row_attend(0)
    project(1)
    col_visit(0)
    pass_on(2)
    row_attend(1)
    project(2)
    col_attend(0)
    col_visit(1)
    pass_on(3)
    finish(0)
    row_attend(2)
    project(3)
    cross(0)
    col_attend(1)
    col_visit(2)
    finish(1)
    row_attend(3)
    cross(1)
    close(0)
    col_visit(3)
    col_attend(2)
    col_attend(3)
    finish(2)
    cross(2)
    close(1)
    finish(3)
    cross(3)
    close(2)
    close(3)

    for group in (x_copies, core_copies, fwd_copies):
        for copy in group:
            copy.wait_send()
    for k in range(chunks):
        column_sends(k, lambda copy: copy.wait_send())
        far_sends(k, lambda copy: copy.wait_send())
        back_copy(k).wait_send()
    for group in (part_copies, cross_copies):
        for copy in group.values():
            copy.wait_send()
    for copy in stores.values():
        copy.wait()


def fused(n, samples, norm_gain, row_qkv, col_qkv, row_out, col_out):
    rows, cols, feat = samples.shape
    chunks = 4
    width = cols // chunks
    half = width // 2
    local = row_qkv.shape[2]
    dma = pltpu.SemaphoreType.DMA
    anywhere = pl.BlockSpec(memory_space=pl.ANY)
    return pl.pallas_call(
        functools.partial(layer_kernel, n, chunks),
        out_shape=jax.ShapeDtypeStruct(samples.shape, samples.dtype),
        in_specs=[anywhere, pl.BlockSpec(memory_space=pltpu.VMEM)] + [anywhere] * 4,
        out_specs=anywhere,
        scratch_shapes=[
            pltpu.VMEM((chunks, 4, rows, width, feat), BF16),
            pltpu.VMEM((6, 4 * feat, local), BF16),
            pltpu.VMEM((4, 2 * local, feat), BF16),
            pltpu.VMEM((rows * width, 4 * feat), BF16),
            pltpu.VMEM((3, rows, cols, local), BF16),
            pltpu.VMEM((chunks, 3, rows, width, local), BF16),
            pltpu.VMEM((chunks, 3, 2 * rows, half, local), BF16),
            pltpu.VMEM((chunks, 2, 2 * rows, half, local), BF16),
            pltpu.VMEM((chunks, 2, 2 * rows, half, local), BF16),
            pltpu.VMEM((chunks, 2, 2 * rows, half, local), BF16),
            pltpu.VMEM((chunks, 2, half // 32, 8, 2 * rows * 32), F32),
            pltpu.VMEM((chunks, 2, 2 * rows, half, local), BF16),
            pltpu.VMEM((chunks, 2, half // 32, 8, 2 * rows * 32), F32),
            pltpu.VMEM((chunks, 2 * rows, half, local), BF16),
            pltpu.VMEM((chunks, rows, width, local), BF16),
            pltpu.VMEM((chunks, rows, width, local), BF16),
            pltpu.VMEM((chunks, 2, rows, width, feat), BF16),
            pltpu.VMEM((chunks, 2, rows, width, feat), BF16),
            pltpu.VMEM((chunks, 2, rows, width, feat), F32),
            pltpu.VMEM((chunks, rows, width, feat), BF16),
            pltpu.VMEM((chunks, rows, width, feat), BF16),
            pltpu.VMEM((chunks, rows, width, feat), BF16),
            dma((10,)),
            dma((chunks,)),
            dma((chunks,)),
            dma((2, chunks)),
            dma((2, chunks)),
            dma((2, chunks)),
            dma((2, chunks, 7)),
            dma((2, chunks, 2, 2)),
            dma((2, chunks)),
            dma((2, chunks, 2)),
            dma((2, chunks)),
        ],
        compiler_params=pltpu.CompilerParams(
            collective_id=0, has_side_effects=True, vmem_limit_bytes=52 * 2**20
        ),
        cost_estimate=pl.CostEstimate(flops=9 * 10**9, bytes_accessed=11 * 2**20, transcendentals=10**6),
    )(samples, norm_gain.reshape(1, -1), row_qkv, col_qkv, row_out, col_out)


def layer_norm(values, norm_gain):
    values = values.astype(F32)
    mean = jnp.mean(values, axis=-1, keepdims=True)
    centred = values - mean
    var = jnp.mean(centred * centred, axis=-1, keepdims=True)
    return (centred * lax.rsqrt(var + 1e-05) * norm_gain).astype(BF16)


def softmax_rounded(scores, allowed):
    scores = jnp.where(allowed, scores, -jnp.inf)
    top = jnp.max(scores, axis=-1, keepdims=True)
    expo = jnp.exp(scores - top)
    return (expo / jnp.sum(expo, axis=-1, keepdims=True)).astype(BF16)


def column_attend(query, keys, vals):
    full_rows = query.shape[0]
    scores = jnp.einsum("qche,kche->chqk", query, keys, preferred_element_type=F32) * (1.0 / HD**0.5)
    allowed = jnp.arange(full_rows)[:, None] >= jnp.arange(full_rows)[None, :]
    weights = softmax_rounded(scores, allowed[None, None])
    return jnp.einsum("chqk,kche->qche", weights, vals, preferred_element_type=F32).astype(BF16)


def unfused(samples, norm_gain, row_qkv, col_qkv, row_out, col_out):
    rows_local, cols, feat_local = samples.shape
    tokens_local = rows_local * cols
    whole = lax.all_gather(samples, "head", axis=2, tiled=True)
    normed = layer_norm(whole, norm_gain).reshape(tokens_local, -1)

    def project(weights):
        mixed = jnp.einsum("nd,tde->tne", normed, weights, preferred_element_type=F32)
        return mixed.astype(BF16).reshape(3, rows_local, cols, -1, HD)

    stacked = project(row_qkv)
    scores = jnp.einsum("rqhe,rkhe->rhqk", stacked[0], stacked[1], preferred_element_type=F32)
    allowed = jnp.arange(cols)[:, None] >= jnp.arange(cols)[None, :]
    weights = softmax_rounded(scores * (1.0 / HD**0.5), allowed[None, None])
    attended = jnp.einsum("rhqk,rkhe->rqhe", weights, stacked[2], preferred_element_type=F32)
    row_attn = attended.astype(BF16).reshape(tokens_local, -1)
    moved = column_attend(
        *(lax.all_to_all(part, "row", split_axis=1, concat_axis=0, tiled=True) for part in project(col_qkv))
    )
    returned = lax.all_to_all(moved, "row", split_axis=0, concat_axis=1, tiled=True)
    partial_term = jnp.dot(row_attn, row_out, preferred_element_type=F32)
    partial_term = partial_term + jnp.dot(
        returned.reshape(tokens_local, -1), col_out, preferred_element_type=F32
    )
    summed = lax.psum_scatter(partial_term.astype(BF16), "head", scatter_dimension=1, tiled=True)
    total = samples.astype(F32) + summed.astype(F32).reshape(rows_local, cols, feat_local)
    return total.astype(BF16)


def solution(mesh):
    n = mesh.shape["row"]

    def shards(samples, *rest):
        if n == 8 and mesh.shape["head"] == 4 and samples.shape[:2] == (2, 512):
            return fused(n, samples, *rest)
        return unfused(samples, *rest)

    placed = (
        P("row", None, "head"),
        P(),
        P(None, None, "head"),
        P(None, None, "head"),
        P("head", None),
        P("head", None),
    )
    return jax.shard_map(
        shards, mesh=mesh, in_specs=placed, out_specs=P("row", None, "head"), check_vma=False
    )
```

```python
import functools

import jax
import jax.numpy as jnp
from jax import lax
from jax.experimental import pallas as pl
from jax.experimental.pallas import tpu as pltpu
from jax.sharding import PartitionSpec as P

HD = 128
LOG2E = 1.4426950408889634
MESH = pl.DeviceIdType.MESH
F32 = jnp.float32
BF16 = jnp.bfloat16


def attend(query, keys, vals, allowed):
    scores = lax.dot_general(query, keys, (((1,), (1,)), ((), ())), preferred_element_type=F32)
    scores = jnp.where(allowed, scores, -jnp.inf)
    expo = jnp.exp2((scores - jnp.max(scores, axis=-1, keepdims=True)) * (LOG2E / HD**0.5))
    total = jnp.sum(expo, axis=-1, keepdims=True)
    out = jnp.dot(expo.astype(BF16), vals, preferred_element_type=F32)
    return (out / total).astype(BF16)


def layer_kernel(
    n, chunks,
    samples, gain_hbm, row_qkv, col_qkv, row_out, col_out, out,
    gain, gathered, wqkv, wout, normed, row_store, col_send, col_recv, col_done, col_back, row_attn,
    part_send, part_recv, kept, cross_send, cross_recv, result,
    load_sem, own_sem, store_sem, x_sem, core_sem, fwd_sem, col_sem, back_sem, part_sem, cross_sem,
):
    rows, cols, feat = samples.shape
    width = cols // chunks
    tokens = rows * width
    each = width // n
    local = row_qkv.shape[2]
    heads = local // HD
    me = lax.axis_index("row")
    head = lax.axis_index("head")
    x_own = head // 2
    core = head % 2
    x_other = 1 - x_own
    core_other = 1 - core
    x_peer = x_other * 2 + core
    core_peer = x_own * 2 + core_other

    def chunk(k):
        return pl.ds(k * width, width)

    loads = [
        pltpu.make_async_copy(row_qkv, wqkv.at[pl.ds(0, 3)], load_sem.at[0]),
        pltpu.make_async_copy(col_qkv, wqkv.at[pl.ds(3, 3)], load_sem.at[1]),
    ]
    own = [
        pltpu.make_async_copy(samples.at[:, chunk(k)], gathered.at[k, head], own_sem.at[k])
        for k in range(chunks)
    ]
    out_loads = []
    for j in range(4):
        for i, ref in enumerate((row_out, col_out)):
            out_loads.append(
                pltpu.make_async_copy(
                    ref.at[:, pl.ds(j * feat, feat)],
                    wout.at[j, pl.ds(i * local, local)],
                    load_sem.at[2 + j * 2 + i],
                )
            )
    gain_load = pltpu.make_async_copy(gain_hbm, gain, load_sem.at[10])
    own[0].start()
    for copy in [gain_load] + loads + own[1:] + out_loads:
        copy.start()

    barrier = pltpu.get_barrier_semaphore()
    pl.semaphore_signal(barrier, inc=1, device_id={"head": x_peer}, device_id_type=MESH)
    pl.semaphore_signal(barrier, inc=1, device_id={"head": core_peer}, device_id_type=MESH)
    for d in range(1, n):
        pl.semaphore_signal(barrier, inc=1, device_id={"row": lax.rem(me + d, n)}, device_id_type=MESH)
    pl.semaphore_wait(barrier, n + 1)

    def remote(src, dst, sems, where, peer):
        return pltpu.make_async_remote_copy(
            src_ref=src, dst_ref=dst, send_sem=sems.at[(0,) + where], recv_sem=sems.at[(1,) + where],
            device_id=peer, device_id_type=MESH,
        )

    x_copies = {
        (k, r): remote(
            samples.at[r, chunk(k)], gathered.at[k, head, r], x_sem, (k, r), {"head": x_peer}
        )
        for k in range(chunks)
        for r in range(rows)
    }
    core_copies = [
        remote(samples.at[:, chunk(k)], gathered.at[k, head], core_sem, (k,), {"head": core_peer})
        for k in range(chunks)
    ]
    fwd_copies = {
        (k, r): remote(
            gathered.at[k, x_peer, r], gathered.at[k, x_peer, r], fwd_sem, (k, r), {"head": core_peer}
        )
        for k in range(chunks)
        for r in range(rows)
    }
    col_copies, back_copies, part_copies, cross_copies, stores = {}, {}, {}, {}, {}

    def send_samples(k):
        if k < chunks:
            for r in range(rows):
                x_copies[k, r].start()
            core_copies[k].start()

    def pass_on(k):
        for r in range(rows):
            x_copies[k, r].wait_recv()
            fwd_copies[k, r].start()
        if k == 0:
            send_samples(1)
        send_samples(k + 2)

    def normalise(k, r):
        step, lane = 64, 128
        tiles = [(j, pl.ds(l * lane, lane), pl.ds(j * feat + l * lane, lane))
                 for j in range(4) for l in range(feat // lane)]
        for i in range(width // step):
            at = pl.ds(i * step, step)
            to = pl.ds(r * width + i * step, step)

            def tile(j, lanes):
                return gathered[k, j, r, at, lanes].astype(F32)

            total = sum(tile(j, lanes) for j, lanes, _ in tiles)
            mean = jnp.sum(total, axis=-1, keepdims=True) * (1.0 / (4 * feat))
            total = sum((tile(j, lanes) - mean) ** 2 for j, lanes, _ in tiles)
            var = jnp.sum(total, axis=-1, keepdims=True) * (1.0 / (4 * feat))
            inv = lax.rsqrt(var + 1e-05)
            for j, lanes, whole in tiles:
                normed[to, whole] = ((tile(j, lanes) - mean) * inv * gain[:, whole]).astype(BF16)

    def project(k):
        own[k].wait()
        core_copies[k].wait_recv()
        if k == 0:
            gain_load.wait()
        for r in range(rows):
            fwd_copies[k, r].wait_recv()
            normalise(k, r)

        if k == 0:
            for copy in loads:
                copy.wait()

        def mixed(t):
            value = jnp.dot(normed[...], wqkv[t], preferred_element_type=F32)
            return value.astype(BF16).reshape(rows, width, local)

        for t in range(3):
            col_send[k, t] = mixed(t + 3)

        for d in range(1, n):
            peer = lax.rem(me + d, n)
            cut = pl.ds(pl.multiple_of(peer * each, each), each)
            col_copies[k, d] = remote(
                col_send.at[k, :, :, cut], col_recv.at[k, me], col_sem, (k, d), {"row": peer}
            )
            col_copies[k, d].start()
        mine = pl.ds(pl.multiple_of(me * each, each), each)
        col_recv[k, me] = col_send[k, :, :, mine, :]

        for t in range(3):
            row_store[t, :, chunk(k), :] = mixed(t)

    def row_attend(k):
        seen = (k + 1) * width
        i = lax.broadcasted_iota(jnp.int32, (width, seen), 0) + k * width
        j = lax.broadcasted_iota(jnp.int32, (width, seen), 1)
        for r in range(rows):
            for h in range(heads):
                lanes = pl.ds(h * HD, HD)
                row_attn[k, r, :, lanes] = attend(
                    row_store[0, r, chunk(k), lanes],
                    row_store[1, r, pl.ds(0, seen), lanes],
                    row_store[2, r, pl.ds(0, seen), lanes],
                    j <= i,
                )

    def col_attend(k):
        for d in range(1, n):
            col_copies[k, d].wait_recv()
        held = n * rows * each
        i = lax.broadcasted_iota(jnp.int32, (held, held), 0)
        j = lax.broadcasted_iota(jnp.int32, (held, held), 1)
        allowed = (j <= i) & (lax.rem(i, each) == lax.rem(j, each))
        for h in range(heads):
            lanes = pl.ds(h * HD, HD)
            parts = [col_recv[k, :, t, :, :, lanes].reshape(held, HD) for t in range(3)]
            col_done[k, :, :, :, lanes] = attend(*parts, allowed).reshape(n, rows, each, HD)
        mine = pl.ds(pl.multiple_of(me * each, each), each)
        for d in range(1, n):
            peer = lax.rem(me + d, n)
            back_copies[k, d] = remote(
                col_done.at[k, peer], col_back.at[k, :, mine], back_sem, (k, d), {"row": peer}
            )
            back_copies[k, d].start()
        col_back[k, :, mine, :] = col_done[k, me]

    def finish(k):
        if k == 0:
            for copy in out_loads:
                copy.wait()
        for d in range(1, n):
            back_copies[k, d].wait_recv()
        attn = jnp.concatenate(
            [row_attn[k].reshape(tokens, local), col_back[k].reshape(tokens, local)], axis=-1
        )

        def block(j):
            return jnp.dot(attn, wout[j], preferred_element_type=F32)

        for s, xb in enumerate((x_other, x_own)):
            part_send[k, s] = block(xb * 2 + core_other).astype(BF16).reshape(rows, width, feat)
            part_copies[k, s] = remote(
                part_send.at[k, s], part_recv.at[k, s], part_sem, (k, s), {"head": core_peer}
            )
            part_copies[k, s].start()
        for s, xb in enumerate((x_other, x_own)):
            kept[k, s] = block(xb * 2 + core).reshape(rows, width, feat)

    def cross(k):
        part_copies[k, 0].wait_recv()
        cross_send[k] = (kept[k, 0] + part_recv[k, 0].astype(F32)).astype(BF16)
        cross_copies[k] = remote(
            cross_send.at[k], cross_recv.at[k], cross_sem, (k,), {"head": x_peer}
        )
        cross_copies[k].start()

    def close(k):
        part_copies[k, 1].wait_recv()
        cross_copies[k].wait_recv()
        total = kept[k, 1] + part_recv[k, 1].astype(F32) + cross_recv[k].astype(F32)
        result[k] = (gathered[k, head].astype(F32) + total).astype(BF16)
        stores[k] = pltpu.make_async_copy(result.at[k], out.at[:, chunk(k)], store_sem.at[k])
        stores[k].start()

    send_samples(0)
    pass_on(0)
    project(0)
    pass_on(1)
    row_attend(0)
    project(1)
    pass_on(2)
    row_attend(1)
    project(2)
    col_attend(0)
    pass_on(3)
    row_attend(2)
    project(3)
    row_attend(3)
    col_attend(1)
    finish(0)
    cross(0)
    col_attend(2)
    finish(1)
    cross(1)
    close(0)
    col_attend(3)
    finish(2)
    cross(2)
    close(1)
    finish(3)
    cross(3)
    close(2)
    close(3)

    for copy in core_copies:
        copy.wait_send()
    for group in (x_copies, fwd_copies, col_copies, back_copies, part_copies, cross_copies):
        for copy in group.values():
            copy.wait_send()
    for copy in stores.values():
        copy.wait()


def fused(n, samples, norm_gain, row_qkv, col_qkv, row_out, col_out):
    rows, cols, feat = samples.shape
    chunks = 4
    width = cols // chunks
    each = width // n
    local = row_qkv.shape[2]
    dma = pltpu.SemaphoreType.DMA
    anywhere = pl.BlockSpec(memory_space=pl.ANY)
    return pl.pallas_call(
        functools.partial(layer_kernel, n, chunks),
        out_shape=jax.ShapeDtypeStruct(samples.shape, samples.dtype),
        in_specs=[anywhere] * 6,
        out_specs=anywhere,
        scratch_shapes=[
            pltpu.VMEM((1, 4 * feat), F32),
            pltpu.VMEM((chunks, 4, rows, width, feat), BF16),
            pltpu.VMEM((6, 4 * feat, local), BF16),
            pltpu.VMEM((4, 2 * local, feat), BF16),
            pltpu.VMEM((rows * width, 4 * feat), BF16),
            pltpu.VMEM((3, rows, cols, local), BF16),
            pltpu.VMEM((chunks, 3, rows, width, local), BF16),
            pltpu.VMEM((chunks, n, 3, rows, each, local), BF16),
            pltpu.VMEM((chunks, n, rows, each, local), BF16),
            pltpu.VMEM((chunks, rows, width, local), BF16),
            pltpu.VMEM((chunks, rows, width, local), BF16),
            pltpu.VMEM((chunks, 2, rows, width, feat), BF16),
            pltpu.VMEM((chunks, 2, rows, width, feat), BF16),
            pltpu.VMEM((chunks, 2, rows, width, feat), F32),
            pltpu.VMEM((chunks, rows, width, feat), BF16),
            pltpu.VMEM((chunks, rows, width, feat), BF16),
            pltpu.VMEM((chunks, rows, width, feat), BF16),
            dma((11,)),
            dma((chunks,)),
            dma((chunks,)),
            dma((2, chunks, rows)),
            dma((2, chunks)),
            dma((2, chunks, rows)),
            dma((2, chunks, n)),
            dma((2, chunks, n)),
            dma((2, chunks, 2)),
            dma((2, chunks)),
        ],
        compiler_params=pltpu.CompilerParams(
            collective_id=0, has_side_effects=True, vmem_limit_bytes=52 * 2**20
        ),
        cost_estimate=pl.CostEstimate(flops=9 * 10**9, bytes_accessed=11 * 2**20, transcendentals=10**6),
    )(samples, norm_gain.reshape(1, -1), row_qkv, col_qkv, row_out, col_out)


def layer_norm(values, norm_gain):
    values = values.astype(F32)
    mean = jnp.mean(values, axis=-1, keepdims=True)
    centred = values - mean
    var = jnp.mean(centred * centred, axis=-1, keepdims=True)
    return (centred * lax.rsqrt(var + 1e-05) * norm_gain).astype(BF16)


def softmax_rounded(scores, allowed):
    scores = jnp.where(allowed, scores, -jnp.inf)
    top = jnp.max(scores, axis=-1, keepdims=True)
    expo = jnp.exp(scores - top)
    return (expo / jnp.sum(expo, axis=-1, keepdims=True)).astype(BF16)


def column_attend(query, keys, vals):
    full_rows = query.shape[0]
    scores = jnp.einsum("qche,kche->chqk", query, keys, preferred_element_type=F32) * (1.0 / HD**0.5)
    allowed = jnp.arange(full_rows)[:, None] >= jnp.arange(full_rows)[None, :]
    weights = softmax_rounded(scores, allowed[None, None])
    return jnp.einsum("chqk,kche->qche", weights, vals, preferred_element_type=F32).astype(BF16)


def unfused(samples, norm_gain, row_qkv, col_qkv, row_out, col_out):
    rows_local, cols, feat_local = samples.shape
    tokens_local = rows_local * cols
    whole = lax.all_gather(samples, "head", axis=2, tiled=True)
    normed = layer_norm(whole, norm_gain).reshape(tokens_local, -1)

    def project(weights):
        mixed = jnp.einsum("nd,tde->tne", normed, weights, preferred_element_type=F32)
        return mixed.astype(BF16).reshape(3, rows_local, cols, -1, HD)

    stacked = project(row_qkv)
    scores = jnp.einsum("rqhe,rkhe->rhqk", stacked[0], stacked[1], preferred_element_type=F32)
    allowed = jnp.arange(cols)[:, None] >= jnp.arange(cols)[None, :]
    weights = softmax_rounded(scores * (1.0 / HD**0.5), allowed[None, None])
    attended = jnp.einsum("rhqk,rkhe->rqhe", weights, stacked[2], preferred_element_type=F32)
    row_attn = attended.astype(BF16).reshape(tokens_local, -1)
    moved = column_attend(
        *(lax.all_to_all(part, "row", split_axis=1, concat_axis=0, tiled=True) for part in project(col_qkv))
    )
    returned = lax.all_to_all(moved, "row", split_axis=0, concat_axis=1, tiled=True)
    partial_term = jnp.dot(row_attn, row_out, preferred_element_type=F32)
    partial_term = partial_term + jnp.dot(
        returned.reshape(tokens_local, -1), col_out, preferred_element_type=F32
    )
    summed = lax.psum_scatter(partial_term.astype(BF16), "head", scatter_dimension=1, tiled=True)
    total = samples.astype(F32) + summed.astype(F32).reshape(rows_local, cols, feat_local)
    return total.astype(BF16)


def solution(mesh):
    n = mesh.shape["row"]

    def shards(samples, *rest):
        if mesh.shape["head"] == 4 and samples.shape[1] % (4 * 16 * n) == 0:
            return fused(n, samples, *rest)
        return unfused(samples, *rest)

    placed = (
        P("row", None, "head"),
        P(),
        P(None, None, "head"),
        P(None, None, "head"),
        P("head", None),
        P("head", None),
    )
    return jax.shard_map(
        shards, mesh=mesh, in_specs=placed, out_specs=P("row", None, "head"), check_vma=False
    )
```

```python
import functools

import jax
import jax.numpy as jnp
from jax import lax
from jax.experimental import pallas as pl
from jax.experimental.pallas import tpu as pltpu
from jax.sharding import PartitionSpec as P

HD = 128
LOG2E = 1.4426950408889634
MESH = pl.DeviceIdType.MESH
F32 = jnp.float32
BF16 = jnp.bfloat16


def attend(query, keys, vals, allowed):
    scores = lax.dot_general(query, keys, (((1,), (1,)), ((), ())), preferred_element_type=F32)
    scores = jnp.where(allowed, scores, -jnp.inf)
    expo = jnp.exp2((scores - jnp.max(scores, axis=-1, keepdims=True)) * (LOG2E / HD**0.5))
    total = jnp.sum(expo, axis=-1, keepdims=True)
    out = jnp.dot(expo.astype(BF16), vals, preferred_element_type=F32)
    return (out / total).astype(BF16)


def layer_kernel(
    n, chunks,
    samples, gain_hbm, row_qkv, col_qkv, row_out, col_out, out,
    gain, gathered, wqkv, wout, normed, row_store, col_send, col_recv, col_done, col_back, row_attn,
    part_send, part_recv, kept, cross_send, cross_recv, result,
    load_sem, own_sem, store_sem, x_sem, core_sem, fwd_sem, col_sem, back_sem, part_sem, cross_sem,
):
    rows, cols, feat = samples.shape
    width = cols // chunks
    tokens = rows * width
    each = width // n
    local = row_qkv.shape[2]
    heads = local // HD
    me = lax.axis_index("row")
    head = lax.axis_index("head")
    x_own = head // 2
    core = head % 2
    x_other = 1 - x_own
    core_other = 1 - core
    x_peer = x_other * 2 + core
    core_peer = x_own * 2 + core_other
    mine = pl.ds(pl.multiple_of(me * each, each), each)

    def chunk(k):
        return pl.ds(pl.multiple_of(k * width, width), width)

    gain_load = pltpu.make_async_copy(gain_hbm, gain, load_sem.at[10])
    loads = [
        pltpu.make_async_copy(row_qkv, wqkv.at[pl.ds(0, 3)], load_sem.at[0]),
        pltpu.make_async_copy(col_qkv, wqkv.at[pl.ds(3, 3)], load_sem.at[1]),
    ]
    out_loads = []
    for j in range(4):
        for i, ref in enumerate((row_out, col_out)):
            out_loads.append(
                pltpu.make_async_copy(
                    ref.at[:, pl.ds(j * feat, feat)],
                    wout.at[j, pl.ds(i * local, local)],
                    load_sem.at[2 + j * 2 + i],
                )
            )

    def own_load(k):
        return pltpu.make_async_copy(samples.at[:, chunk(k)], gathered.at[k, head], own_sem.at[k])

    for k in range(chunks):
        own_load(k).start()
    for copy in [gain_load] + loads + out_loads:
        copy.start()

    barrier = pltpu.get_barrier_semaphore()
    pl.semaphore_signal(barrier, inc=1, device_id={"head": x_peer}, device_id_type=MESH)
    pl.semaphore_signal(barrier, inc=1, device_id={"head": core_peer}, device_id_type=MESH)
    for d in range(1, n):
        pl.semaphore_signal(barrier, inc=1, device_id={"row": lax.rem(me + d, n)}, device_id_type=MESH)
    pl.semaphore_wait(barrier, n + 1)

    def remote(src, dst, sems, where, peer):
        return pltpu.make_async_remote_copy(
            src_ref=src, dst_ref=dst, send_sem=sems.at[(0,) + where], recv_sem=sems.at[(1,) + where],
            device_id=peer, device_id_type=MESH,
        )

    def x_copy(k, r):
        return remote(
            samples.at[r, chunk(k)], gathered.at[k, head, r], x_sem, (k, r), {"head": x_peer}
        )

    def core_copy(k):
        return remote(
            samples.at[:, chunk(k)], gathered.at[k, head], core_sem, (k,), {"head": core_peer}
        )

    def fwd_copy(k, r):
        return remote(
            gathered.at[k, x_peer, r], gathered.at[k, x_peer, r], fwd_sem, (k, r), {"head": core_peer}
        )

    def col_copy(k, d):
        peer = lax.rem(me + d, n)
        cut = pl.ds(pl.multiple_of(peer * each, each), each)
        return remote(
            col_send.at[k, :, :, cut], col_recv.at[k, me], col_sem, (k, d), {"row": peer}
        )

    def back_copy(k, d):
        peer = lax.rem(me + d, n)
        return remote(
            col_done.at[k, peer], col_back.at[k, :, mine], back_sem, (k, d), {"row": peer}
        )

    def part_copy(k, s):
        return remote(part_send.at[k, s], part_recv.at[k, s], part_sem, (k, s), {"head": core_peer})

    def cross_copy(k):
        return remote(cross_send.at[k], cross_recv.at[k], cross_sem, (k,), {"head": x_peer})

    def store(k):
        return pltpu.make_async_copy(result.at[k], out.at[:, chunk(k)], store_sem.at[k])

    def send_samples(k):
        for r in range(rows):
            x_copy(k, r).start()
        core_copy(k).start()

    def pass_on(k):
        for r in range(rows):
            x_copy(k, r).wait_recv()
            fwd_copy(k, r).start()

        @pl.when(k == 0)
        def _():
            send_samples(1)

        @pl.when(k + 2 < chunks)
        def _():
            send_samples(k + 2)

    def normalise(k, r):
        step, lane = 64, 128
        tiles = [(j, pl.ds(l * lane, lane), pl.ds(j * feat + l * lane, lane))
                 for j in range(4) for l in range(feat // lane)]
        for i in range(width // step):
            at = pl.ds(i * step, step)
            to = pl.ds(pl.multiple_of(r * width + i * step, step), step)

            def tile(j, lanes):
                return gathered[k, j, r, at, lanes].astype(F32)

            total = sum(tile(j, lanes) for j, lanes, _ in tiles)
            mean = jnp.sum(total, axis=-1, keepdims=True) * (1.0 / (4 * feat))
            total = sum((tile(j, lanes) - mean) ** 2 for j, lanes, _ in tiles)
            var = jnp.sum(total, axis=-1, keepdims=True) * (1.0 / (4 * feat))
            inv = lax.rsqrt(var + 1e-05)
            for j, lanes, whole in tiles:
                normed[to, whole] = ((tile(j, lanes) - mean) * inv * gain[:, whole]).astype(BF16)

    def project(k):
        own_load(k).wait()
        core_copy(k).wait_recv()

        @pl.when(k == 0)
        def _():
            gain_load.wait()

        @pl.loop(0, rows)
        def _(r):
            fwd_copy(k, r).wait_recv()
            normalise(k, r)

        @pl.when(k == 0)
        def _():
            for copy in loads:
                copy.wait()

        def mixed(t):
            value = jnp.dot(normed[...], wqkv[t], preferred_element_type=F32)
            return value.astype(BF16).reshape(rows, width, local)

        @pl.loop(0, 3)
        def _(t):
            col_send[k, t] = mixed(t + 3)

        @pl.loop(1, n)
        def _(d):
            col_copy(k, d).start()

        col_recv[k, me] = col_send[k, :, :, mine, :]

        @pl.loop(0, 3)
        def _(t):
            row_store[t, :, chunk(k), :] = mixed(t)

    def row_attend(k):
        i = lax.broadcasted_iota(jnp.int32, (width, cols), 0) + k * width
        j = lax.broadcasted_iota(jnp.int32, (width, cols), 1)

        @pl.loop(0, rows)
        def _(r):
            for h in range(heads):
                lanes = pl.ds(h * HD, HD)
                row_attn[k, r, :, lanes] = attend(
                    row_store[0, r, chunk(k), lanes],
                    row_store[1, r, :, lanes],
                    row_store[2, r, :, lanes],
                    j <= i,
                )

    def col_attend(k):
        @pl.loop(1, n)
        def _(d):
            col_copy(k, d).wait_recv()

        held = n * rows * each
        i = lax.broadcasted_iota(jnp.int32, (held, held), 0)
        j = lax.broadcasted_iota(jnp.int32, (held, held), 1)
        allowed = (j <= i) & (lax.rem(i, each) == lax.rem(j, each))
        for h in range(heads):
            lanes = pl.ds(h * HD, HD)
            parts = [col_recv[k, :, t, :, :, lanes].reshape(held, HD) for t in range(3)]
            col_done[k, :, :, :, lanes] = attend(*parts, allowed).reshape(n, rows, each, HD)

        @pl.loop(1, n)
        def _(d):
            back_copy(k, d).start()

        col_back[k, :, mine, :] = col_done[k, me]

    def finish(k):
        @pl.when(k == 0)
        def _():
            for copy in out_loads:
                copy.wait()

        @pl.loop(1, n)
        def _(d):
            back_copy(k, d).wait_recv()

        attn = jnp.concatenate(
            [row_attn[k].reshape(tokens, local), col_back[k].reshape(tokens, local)], axis=-1
        )

        def block(j):
            return jnp.dot(attn, wout[j], preferred_element_type=F32).reshape(rows, width, feat)

        for s, xb in enumerate((x_other, x_own)):
            part_send[k, s] = block(xb * 2 + core_other).astype(BF16)
            part_copy(k, s).start()
        for s, xb in enumerate((x_other, x_own)):
            kept[k, s] = block(xb * 2 + core)

    def cross(k):
        part_copy(k, 0).wait_recv()
        cross_send[k] = (kept[k, 0] + part_recv[k, 0].astype(F32)).astype(BF16)
        cross_copy(k).start()

    def close(k):
        part_copy(k, 1).wait_recv()
        cross_copy(k).wait_recv()
        total = kept[k, 1] + part_recv[k, 1].astype(F32) + cross_recv[k].astype(F32)
        result[k] = (gathered[k, head].astype(F32) + total).astype(BF16)
        store(k).start()

    send_samples(0)
    row_store[1:] = jnp.zeros((2, rows, cols, local), BF16)

    @pl.loop(0, chunks + 2)
    def _(step):
        def stage(action, lag):
            @pl.when((step >= lag) & (step < chunks + lag))
            def _():
                action(step - lag)

        stage(pass_on, 0)
        stage(col_attend, 1)
        stage(project, 0)
        stage(finish, 1)
        stage(row_attend, 0)
        stage(cross, 1)
        stage(close, 2)

    @pl.loop(0, chunks)
    def _(k):
        for r in range(rows):
            x_copy(k, r).wait_send()
            fwd_copy(k, r).wait_send()
        core_copy(k).wait_send()

        @pl.loop(1, n)
        def _(d):
            col_copy(k, d).wait_send()
            back_copy(k, d).wait_send()

        for s in range(2):
            part_copy(k, s).wait_send()
        cross_copy(k).wait_send()
        store(k).wait()


def fused(n, samples, norm_gain, row_qkv, col_qkv, row_out, col_out):
    rows, cols, feat = samples.shape
    chunks = 4
    width = cols // chunks
    each = width // n
    local = row_qkv.shape[2]
    dma = pltpu.SemaphoreType.DMA
    anywhere = pl.BlockSpec(memory_space=pl.ANY)
    return pl.pallas_call(
        functools.partial(layer_kernel, n, chunks),
        out_shape=jax.ShapeDtypeStruct(samples.shape, samples.dtype),
        in_specs=[anywhere] * 6,
        out_specs=anywhere,
        scratch_shapes=[
            pltpu.VMEM((1, 4 * feat), F32),
            pltpu.VMEM((chunks, 4, rows, width, feat), BF16),
            pltpu.VMEM((6, 4 * feat, local), BF16),
            pltpu.VMEM((4, 2 * local, feat), BF16),
            pltpu.VMEM((rows * width, 4 * feat), BF16),
            pltpu.VMEM((3, rows, cols, local), BF16),
            pltpu.VMEM((chunks, 3, rows, width, local), BF16),
            pltpu.VMEM((chunks, n, 3, rows, each, local), BF16),
            pltpu.VMEM((chunks, n, rows, each, local), BF16),
            pltpu.VMEM((chunks, rows, width, local), BF16),
            pltpu.VMEM((chunks, rows, width, local), BF16),
            pltpu.VMEM((chunks, 2, rows, width, feat), BF16),
            pltpu.VMEM((chunks, 2, rows, width, feat), BF16),
            pltpu.VMEM((chunks, 2, rows, width, feat), F32),
            pltpu.VMEM((chunks, rows, width, feat), BF16),
            pltpu.VMEM((chunks, rows, width, feat), BF16),
            pltpu.VMEM((chunks, rows, width, feat), BF16),
            dma((11,)),
            dma((chunks,)),
            dma((chunks,)),
            dma((2, chunks, rows)),
            dma((2, chunks)),
            dma((2, chunks, rows)),
            dma((2, chunks, n)),
            dma((2, chunks, n)),
            dma((2, chunks, 2)),
            dma((2, chunks)),
        ],
        compiler_params=pltpu.CompilerParams(
            collective_id=0, has_side_effects=True, vmem_limit_bytes=52 * 2**20
        ),
        cost_estimate=pl.CostEstimate(flops=9 * 10**9, bytes_accessed=11 * 2**20, transcendentals=10**6),
    )(samples, norm_gain.reshape(1, -1), row_qkv, col_qkv, row_out, col_out)


def layer_norm(values, norm_gain):
    values = values.astype(F32)
    mean = jnp.mean(values, axis=-1, keepdims=True)
    centred = values - mean
    var = jnp.mean(centred * centred, axis=-1, keepdims=True)
    return (centred * lax.rsqrt(var + 1e-05) * norm_gain).astype(BF16)


def softmax_rounded(scores, allowed):
    scores = jnp.where(allowed, scores, -jnp.inf)
    top = jnp.max(scores, axis=-1, keepdims=True)
    expo = jnp.exp(scores - top)
    return (expo / jnp.sum(expo, axis=-1, keepdims=True)).astype(BF16)


def column_attend(query, keys, vals):
    full_rows = query.shape[0]
    scores = jnp.einsum("qche,kche->chqk", query, keys, preferred_element_type=F32) * (1.0 / HD**0.5)
    allowed = jnp.arange(full_rows)[:, None] >= jnp.arange(full_rows)[None, :]
    weights = softmax_rounded(scores, allowed[None, None])
    return jnp.einsum("chqk,kche->qche", weights, vals, preferred_element_type=F32).astype(BF16)


def unfused(samples, norm_gain, row_qkv, col_qkv, row_out, col_out):
    rows_local, cols, feat_local = samples.shape
    tokens_local = rows_local * cols
    whole = lax.all_gather(samples, "head", axis=2, tiled=True)
    normed = layer_norm(whole, norm_gain).reshape(tokens_local, -1)

    def project(weights):
        mixed = jnp.einsum("nd,tde->tne", normed, weights, preferred_element_type=F32)
        return mixed.astype(BF16).reshape(3, rows_local, cols, -1, HD)

    stacked = project(row_qkv)
    scores = jnp.einsum("rqhe,rkhe->rhqk", stacked[0], stacked[1], preferred_element_type=F32)
    allowed = jnp.arange(cols)[:, None] >= jnp.arange(cols)[None, :]
    weights = softmax_rounded(scores * (1.0 / HD**0.5), allowed[None, None])
    attended = jnp.einsum("rhqk,rkhe->rqhe", weights, stacked[2], preferred_element_type=F32)
    row_attn = attended.astype(BF16).reshape(tokens_local, -1)
    moved = column_attend(
        *(lax.all_to_all(part, "row", split_axis=1, concat_axis=0, tiled=True) for part in project(col_qkv))
    )
    returned = lax.all_to_all(moved, "row", split_axis=0, concat_axis=1, tiled=True)
    partial_term = jnp.dot(row_attn, row_out, preferred_element_type=F32)
    partial_term = partial_term + jnp.dot(
        returned.reshape(tokens_local, -1), col_out, preferred_element_type=F32
    )
    summed = lax.psum_scatter(partial_term.astype(BF16), "head", scatter_dimension=1, tiled=True)
    total = samples.astype(F32) + summed.astype(F32).reshape(rows_local, cols, feat_local)
    return total.astype(BF16)


def solution(mesh):
    n = mesh.shape["row"]

    def shards(samples, *rest):
        if mesh.shape["head"] == 4 and samples.shape[1] % (4 * 16 * n) == 0:
            return fused(n, samples, *rest)
        return unfused(samples, *rest)

    placed = (
        P("row", None, "head"),
        P(),
        P(None, None, "head"),
        P(None, None, "head"),
        P("head", None),
        P("head", None),
    )
    return jax.shard_map(
        shards, mesh=mesh, in_specs=placed, out_specs=P("row", None, "head"), check_vma=False
    )
```

```python
import functools

import jax
import jax.numpy as jnp
from jax import lax
from jax.experimental import pallas as pl
from jax.experimental.pallas import tpu as pltpu
from jax.sharding import PartitionSpec as P

HD = 128
LOG2E = 1.4426950408889634
MESH = pl.DeviceIdType.MESH
F32 = jnp.float32
BF16 = jnp.bfloat16


def attend(query, keys, vals, allowed):
    scores = lax.dot_general(query, keys, (((1,), (1,)), ((), ())), preferred_element_type=F32)
    scores = jnp.where(allowed, scores, -jnp.inf)
    expo = jnp.exp2((scores - jnp.max(scores, axis=-1, keepdims=True)) * (LOG2E / HD**0.5))
    total = jnp.sum(expo, axis=-1, keepdims=True)
    out = jnp.dot(expo.astype(BF16), vals, preferred_element_type=F32)
    return (out / total).astype(BF16)


def layer_kernel(
    n, chunks,
    samples, gain_hbm, row_qkv, col_qkv, row_out, col_out, out,
    gain, gathered, wqkv, wout, normed, row_store, col_send, col_recv, col_done, col_back, row_attn,
    low_own, low_done, part_send, part_recv, kept, cross_send, cross_recv, result,
    load_sem, own_sem, store_sem, x_sem, core_sem, fwd_sem, col_sem, back_sem, low_sem, part_sem, cross_sem,
):
    rows, cols, feat = samples.shape
    width = cols // chunks
    tokens = rows * width
    each = width // n
    local = row_qkv.shape[2]
    heads = local // HD
    half = width // 2
    me = lax.axis_index("row")
    z = me // 2
    y = me % 2
    y_other = 1 - y
    y_peer = {"row": z * 2 + y_other}
    head = lax.axis_index("head")
    x_own = head // 2
    core = head % 2
    x_other = 1 - x_own
    core_other = 1 - core
    x_peer = x_other * 2 + core
    core_peer = x_own * 2 + core_other

    def chunk(k):
        return pl.ds(k * width, width)

    loads = [
        pltpu.make_async_copy(row_qkv, wqkv.at[pl.ds(0, 3)], load_sem.at[0]),
        pltpu.make_async_copy(col_qkv, wqkv.at[pl.ds(3, 3)], load_sem.at[1]),
    ]
    own = [
        pltpu.make_async_copy(samples.at[:, chunk(k)], gathered.at[k, head], own_sem.at[k])
        for k in range(chunks)
    ]
    out_loads = []
    for j in range(4):
        for i, ref in enumerate((row_out, col_out)):
            out_loads.append(
                pltpu.make_async_copy(
                    ref.at[:, pl.ds(j * feat, feat)],
                    wout.at[j, pl.ds(i * local, local)],
                    load_sem.at[2 + j * 2 + i],
                )
            )
    gain_load = pltpu.make_async_copy(gain_hbm, gain, load_sem.at[10])
    own[0].start()
    for copy in [gain_load] + loads + own[1:] + out_loads:
        copy.start()

    barrier = pltpu.get_barrier_semaphore()
    pl.semaphore_signal(barrier, inc=1, device_id={"head": x_peer}, device_id_type=MESH)
    pl.semaphore_signal(barrier, inc=1, device_id={"head": core_peer}, device_id_type=MESH)
    for d in range(1, n):
        pl.semaphore_signal(barrier, inc=1, device_id={"row": lax.rem(me + d, n)}, device_id_type=MESH)
    pl.semaphore_wait(barrier, n + 1)

    def remote(src, dst, sems, where, peer):
        return pltpu.make_async_remote_copy(
            src_ref=src, dst_ref=dst, send_sem=sems.at[(0,) + where], recv_sem=sems.at[(1,) + where],
            device_id=peer, device_id_type=MESH,
        )

    x_copies = {
        (k, r): remote(
            samples.at[r, chunk(k)], gathered.at[k, head, r], x_sem, (k, r), {"head": x_peer}
        )
        for k in range(chunks)
        for r in range(rows)
    }
    core_copies = [
        remote(samples.at[:, chunk(k)], gathered.at[k, head], core_sem, (k,), {"head": core_peer})
        for k in range(chunks)
    ]
    fwd_copies = {
        (k, r): remote(
            gathered.at[k, x_peer, r], gathered.at[k, x_peer, r], fwd_sem, (k, r), {"head": core_peer}
        )
        for k in range(chunks)
        for r in range(rows)
    }
    part_copies, cross_copies, stores = {}, {}, {}

    def send_samples(k):
        if k < chunks:
            for r in range(rows):
                x_copies[k, r].start()
            core_copies[k].start()

    def pass_on(k):
        for r in range(rows):
            x_copies[k, r].wait_recv()
            fwd_copies[k, r].start()
        if k == 0:
            send_samples(1)
        send_samples(k + 2)

    def normalise(k, r):
        step, lane = 64, 128
        tiles = [(j, pl.ds(l * lane, lane), pl.ds(j * feat + l * lane, lane))
                 for j in range(4) for l in range(feat // lane)]
        for i in range(width // step):
            at = pl.ds(i * step, step)
            to = pl.ds(r * width + i * step, step)

            def tile(j, lanes):
                return gathered[k, j, r, at, lanes].astype(F32)

            total = sum(tile(j, lanes) for j, lanes, _ in tiles)
            mean = jnp.sum(total, axis=-1, keepdims=True) * (1.0 / (4 * feat))
            total = sum((tile(j, lanes) - mean) ** 2 for j, lanes, _ in tiles)
            var = jnp.sum(total, axis=-1, keepdims=True) * (1.0 / (4 * feat))
            inv = lax.rsqrt(var + 1e-05)
            for j, lanes, whole in tiles:
                normed[to, whole] = ((tile(j, lanes) - mean) * inv * gain[:, whole]).astype(BF16)

    def project(k):
        own[k].wait()
        core_copies[k].wait_recv()
        if k == 0:
            gain_load.wait()
        for r in range(rows):
            fwd_copies[k, r].wait_recv()
            normalise(k, r)

        if k == 0:
            for copy in loads:
                copy.wait()

        def mixed(t):
            value = jnp.dot(normed[...], wqkv[t], preferred_element_type=F32)
            return value.astype(BF16).reshape(rows, width, local)

        for t in range(3):
            col_send[k, t] = mixed(t + 3)

        column_sends(k, lambda copy: copy.start())
        col_recv[k, me] = col_send[k, :, :, mine, :]

        @pl.when(z == 0)
        def _():
            low_own[k, :, pl.ds(y * rows, rows)] = col_send[k, :, :, my_half, :]

        for t in range(3):
            row_store[t, :, chunk(k), :] = mixed(t)

    def row_attend(k):
        seen = (k + 1) * width
        i = lax.broadcasted_iota(jnp.int32, (width, seen), 0) + k * width
        j = lax.broadcasted_iota(jnp.int32, (width, seen), 1)
        for r in range(rows):
            for h in range(heads):
                lanes = pl.ds(h * HD, HD)
                row_attn[k, r, :, lanes] = attend(
                    row_store[0, r, chunk(k), lanes],
                    row_store[1, r, pl.ds(0, seen), lanes],
                    row_store[2, r, pl.ds(0, seen), lanes],
                    j <= i,
                )

    mine = pl.ds(pl.multiple_of(me * each, each), each)
    my_half = pl.ds(pl.multiple_of(y * half, half), half)
    their_half = pl.ds(pl.multiple_of(y_other * half, half), half)

    def col_copy(k, d, first):
        peer = lax.rem(me + d, n)
        cut = pl.ds(pl.multiple_of(peer * each, each), each)
        kinds = pl.ds(first, 3 - first)
        return remote(
            col_send.at[k, kinds, :, cut], col_recv.at[k, me, kinds], col_sem, (k, d), {"row": peer}
        )

    def low_copy(k):
        return remote(
            col_send.at[k, :, :, their_half], low_own.at[k, :, pl.ds(y * rows, rows)],
            low_sem, (k, 0), y_peer,
        )

    def low_back(k):
        return remote(
            low_done.at[k, pl.ds(y_other * rows, rows)], col_back.at[k, :, my_half],
            low_sem, (k, 1), y_peer,
        )

    def back_copy(k, d):
        peer = lax.rem(me + d, n)
        return remote(
            col_done.at[k, peer], col_back.at[k, :, mine], back_sem, (k, d), {"row": peer}
        )

    def column_sends(k, act):
        @pl.when(z == 0)
        def _():
            act(low_copy(k))
            for d in range(1, n):
                act(col_copy(k, d, 1))

        @pl.when(z > 0)
        def _():
            for d in range(1, n):
                act(col_copy(k, d, 0))

    def back_sends(k, act):
        for d in range(1, n):

            @pl.when(lax.rem(me + d, n) >= 2)
            def _(d=d):
                act(back_copy(k, d))

    def columns_arrive(k):
        for d in range(1, n):
            source = lax.rem(me + n - d, n)

            @pl.when(source < 2)
            def _(d=d):
                col_copy(k, d, 1).wait_recv()

            @pl.when(source >= 2)
            def _(d=d):
                col_copy(k, d, 0).wait_recv()

    def low_attend(k):
        low_copy(k).wait_recv()
        band = 32
        held = 2 * rows * band
        i = lax.broadcasted_iota(jnp.int32, (held, held), 0)
        j = lax.broadcasted_iota(jnp.int32, (held, held), 1)
        allowed = (j <= i) & (lax.rem(i, band) == lax.rem(j, band))
        for b in range(half // band):
            cut = pl.ds(b * band, band)
            for h in range(heads):
                lanes = pl.ds(h * HD, HD)
                parts = [low_own[k, t, :, cut, lanes].reshape(held, HD) for t in range(3)]
                low_done[k, :, cut, lanes] = attend(*parts, allowed).reshape(2 * rows, band, HD)
        low_back(k).start()
        col_back[k, :, my_half, :] = low_done[k, pl.ds(y * rows, rows)]

    def col_attend(k):
        @pl.when(z == 0)
        def _():
            low_attend(k)

        columns_arrive(k)
        held = n * rows * each
        asking = (n - 2) * rows * each
        i = lax.broadcasted_iota(jnp.int32, (asking, held), 0) + (held - asking)
        j = lax.broadcasted_iota(jnp.int32, (asking, held), 1)
        allowed = (j <= i) & (lax.rem(i, each) == lax.rem(j, each))
        for h in range(heads):
            lanes = pl.ds(h * HD, HD)
            query = col_recv[k, 2:, 0, :, :, lanes].reshape(asking, HD)
            parts = [col_recv[k, :, t, :, :, lanes].reshape(held, HD) for t in (1, 2)]
            col_done[k, 2:, :, :, lanes] = attend(query, *parts, allowed).reshape(n - 2, rows, each, HD)
        back_sends(k, lambda copy: copy.start())

        @pl.when(z > 0)
        def _():
            col_back[k, :, mine, :] = col_done[k, me]

    def finish(k):
        if k == 0:
            for copy in out_loads:
                copy.wait()

        @pl.when(z == 0)
        def _():
            low_back(k).wait_recv()

        @pl.when(z > 0)
        def _():
            for d in range(1, n):
                back_copy(k, d).wait_recv()

        attn = jnp.concatenate(
            [row_attn[k].reshape(tokens, local), col_back[k].reshape(tokens, local)], axis=-1
        )

        def block(j):
            return jnp.dot(attn, wout[j], preferred_element_type=F32)

        for s, xb in enumerate((x_other, x_own)):
            part_send[k, s] = block(xb * 2 + core_other).astype(BF16).reshape(rows, width, feat)
            part_copies[k, s] = remote(
                part_send.at[k, s], part_recv.at[k, s], part_sem, (k, s), {"head": core_peer}
            )
            part_copies[k, s].start()
        for s, xb in enumerate((x_other, x_own)):
            kept[k, s] = block(xb * 2 + core).reshape(rows, width, feat)

    def cross(k):
        part_copies[k, 0].wait_recv()
        cross_send[k] = (kept[k, 0] + part_recv[k, 0].astype(F32)).astype(BF16)
        cross_copies[k] = remote(
            cross_send.at[k], cross_recv.at[k], cross_sem, (k,), {"head": x_peer}
        )
        cross_copies[k].start()

    def close(k):
        part_copies[k, 1].wait_recv()
        cross_copies[k].wait_recv()
        total = kept[k, 1] + part_recv[k, 1].astype(F32) + cross_recv[k].astype(F32)
        result[k] = (gathered[k, head].astype(F32) + total).astype(BF16)
        stores[k] = pltpu.make_async_copy(result.at[k], out.at[:, chunk(k)], store_sem.at[k])
        stores[k].start()

    send_samples(0)
    pass_on(0)
    project(0)
    pass_on(1)
    row_attend(0)
    project(1)
    pass_on(2)
    row_attend(1)
    project(2)
    col_attend(0)
    pass_on(3)
    row_attend(2)
    project(3)
    finish(0)
    row_attend(3)
    cross(0)
    col_attend(1)
    close(0)
    col_attend(2)
    finish(1)
    cross(1)
    col_attend(3)
    finish(2)
    cross(2)
    close(1)
    finish(3)
    cross(3)
    close(2)
    close(3)

    for copy in core_copies:
        copy.wait_send()
    for k in range(chunks):
        column_sends(k, lambda copy: copy.wait_send())
        back_sends(k, lambda copy: copy.wait_send())

        @pl.when(z == 0)
        def _(k=k):
            low_back(k).wait_send()

    for group in (x_copies, fwd_copies, part_copies, cross_copies):
        for copy in group.values():
            copy.wait_send()
    for copy in stores.values():
        copy.wait()


def fused(n, samples, norm_gain, row_qkv, col_qkv, row_out, col_out):
    rows, cols, feat = samples.shape
    chunks = 4
    width = cols // chunks
    each = width // n
    local = row_qkv.shape[2]
    dma = pltpu.SemaphoreType.DMA
    anywhere = pl.BlockSpec(memory_space=pl.ANY)
    return pl.pallas_call(
        functools.partial(layer_kernel, n, chunks),
        out_shape=jax.ShapeDtypeStruct(samples.shape, samples.dtype),
        in_specs=[anywhere] * 6,
        out_specs=anywhere,
        scratch_shapes=[
            pltpu.VMEM((1, 4 * feat), F32),
            pltpu.VMEM((chunks, 4, rows, width, feat), BF16),
            pltpu.VMEM((6, 4 * feat, local), BF16),
            pltpu.VMEM((4, 2 * local, feat), BF16),
            pltpu.VMEM((rows * width, 4 * feat), BF16),
            pltpu.VMEM((3, rows, cols, local), BF16),
            pltpu.VMEM((chunks, 3, rows, width, local), BF16),
            pltpu.VMEM((chunks, n, 3, rows, each, local), BF16),
            pltpu.VMEM((chunks, n, rows, each, local), BF16),
            pltpu.VMEM((chunks, rows, width, local), BF16),
            pltpu.VMEM((chunks, rows, width, local), BF16),
            pltpu.VMEM((chunks, 3, 2 * rows, width // 2, local), BF16),
            pltpu.VMEM((chunks, 2 * rows, width // 2, local), BF16),
            pltpu.VMEM((chunks, 2, rows, width, feat), BF16),
            pltpu.VMEM((chunks, 2, rows, width, feat), BF16),
            pltpu.VMEM((chunks, 2, rows, width, feat), F32),
            pltpu.VMEM((chunks, rows, width, feat), BF16),
            pltpu.VMEM((chunks, rows, width, feat), BF16),
            pltpu.VMEM((chunks, rows, width, feat), BF16),
            dma((11,)),
            dma((chunks,)),
            dma((chunks,)),
            dma((2, chunks, rows)),
            dma((2, chunks)),
            dma((2, chunks, rows)),
            dma((2, chunks, n)),
            dma((2, chunks, n)),
            dma((2, chunks, 2)),
            dma((2, chunks, 2)),
            dma((2, chunks)),
        ],
        compiler_params=pltpu.CompilerParams(
            collective_id=0, has_side_effects=True, vmem_limit_bytes=52 * 2**20
        ),
        cost_estimate=pl.CostEstimate(flops=9 * 10**9, bytes_accessed=11 * 2**20, transcendentals=10**6),
    )(samples, norm_gain.reshape(1, -1), row_qkv, col_qkv, row_out, col_out)


def layer_norm(values, norm_gain):
    values = values.astype(F32)
    mean = jnp.mean(values, axis=-1, keepdims=True)
    centred = values - mean
    var = jnp.mean(centred * centred, axis=-1, keepdims=True)
    return (centred * lax.rsqrt(var + 1e-05) * norm_gain).astype(BF16)


def softmax_rounded(scores, allowed):
    scores = jnp.where(allowed, scores, -jnp.inf)
    top = jnp.max(scores, axis=-1, keepdims=True)
    expo = jnp.exp(scores - top)
    return (expo / jnp.sum(expo, axis=-1, keepdims=True)).astype(BF16)


def column_attend(query, keys, vals):
    full_rows = query.shape[0]
    scores = jnp.einsum("qche,kche->chqk", query, keys, preferred_element_type=F32) * (1.0 / HD**0.5)
    allowed = jnp.arange(full_rows)[:, None] >= jnp.arange(full_rows)[None, :]
    weights = softmax_rounded(scores, allowed[None, None])
    return jnp.einsum("chqk,kche->qche", weights, vals, preferred_element_type=F32).astype(BF16)


def unfused(samples, norm_gain, row_qkv, col_qkv, row_out, col_out):
    rows_local, cols, feat_local = samples.shape
    tokens_local = rows_local * cols
    whole = lax.all_gather(samples, "head", axis=2, tiled=True)
    normed = layer_norm(whole, norm_gain).reshape(tokens_local, -1)

    def project(weights):
        mixed = jnp.einsum("nd,tde->tne", normed, weights, preferred_element_type=F32)
        return mixed.astype(BF16).reshape(3, rows_local, cols, -1, HD)

    stacked = project(row_qkv)
    scores = jnp.einsum("rqhe,rkhe->rhqk", stacked[0], stacked[1], preferred_element_type=F32)
    allowed = jnp.arange(cols)[:, None] >= jnp.arange(cols)[None, :]
    weights = softmax_rounded(scores * (1.0 / HD**0.5), allowed[None, None])
    attended = jnp.einsum("rhqk,rkhe->rqhe", weights, stacked[2], preferred_element_type=F32)
    row_attn = attended.astype(BF16).reshape(tokens_local, -1)
    moved = column_attend(
        *(lax.all_to_all(part, "row", split_axis=1, concat_axis=0, tiled=True) for part in project(col_qkv))
    )
    returned = lax.all_to_all(moved, "row", split_axis=0, concat_axis=1, tiled=True)
    partial_term = jnp.dot(row_attn, row_out, preferred_element_type=F32)
    partial_term = partial_term + jnp.dot(
        returned.reshape(tokens_local, -1), col_out, preferred_element_type=F32
    )
    summed = lax.psum_scatter(partial_term.astype(BF16), "head", scatter_dimension=1, tiled=True)
    total = samples.astype(F32) + summed.astype(F32).reshape(rows_local, cols, feat_local)
    return total.astype(BF16)


def solution(mesh):
    n = mesh.shape["row"]

    def shards(samples, *rest):
        if n == 8 and mesh.shape["head"] == 4 and samples.shape[:2] == (2, 512):
            return fused(n, samples, *rest)
        return unfused(samples, *rest)

    placed = (
        P("row", None, "head"),
        P(),
        P(None, None, "head"),
        P(None, None, "head"),
        P("head", None),
        P("head", None),
    )
    return jax.shard_map(
        shards, mesh=mesh, in_specs=placed, out_specs=P("row", None, "head"), check_vma=False
    )
```

```python
import functools

import jax
import jax.numpy as jnp
from jax import lax
from jax.experimental import pallas as pl
from jax.experimental.pallas import tpu as pltpu
from jax.sharding import PartitionSpec as P

HD = 128
LOG2E = 1.4426950408889634
MESH = pl.DeviceIdType.MESH
F32 = jnp.float32
BF16 = jnp.bfloat16


def attend(query, keys, vals, allowed):
    scores = lax.dot_general(query, keys, (((1,), (1,)), ((), ())), preferred_element_type=F32)
    scores = jnp.where(allowed, scores, -jnp.inf)
    expo = jnp.exp2((scores - jnp.max(scores, axis=-1, keepdims=True)) * (LOG2E / HD**0.5))
    total = jnp.sum(expo, axis=-1, keepdims=True)
    out = jnp.dot(expo.astype(BF16), vals, preferred_element_type=F32)
    return (out / total).astype(BF16)


def layer_kernel(
    n, chunks,
    samples, gain_hbm, row_qkv, col_qkv, row_out, col_out, out,
    gain, gathered, wqkv, wout, normed, row_store, col_send, col_recv, col_done, col_back, row_attn,
    part_send, part_recv, kept, cross_send, cross_recv, result,
    load_sem, own_sem, store_sem, x_sem, core_sem, fwd_sem, col_sem, back_sem, part_sem, cross_sem,
):
    rows, cols, feat = samples.shape
    width = cols // chunks
    tokens = rows * width
    each = width // n
    local = row_qkv.shape[2]
    heads = local // HD
    me = lax.axis_index("row")
    head = lax.axis_index("head")
    x_own = head // 2
    core = head % 2
    x_other = 1 - x_own
    core_other = 1 - core
    x_peer = x_other * 2 + core
    core_peer = x_own * 2 + core_other

    def chunk(k):
        return pl.ds(k * width, width)

    loads = [
        pltpu.make_async_copy(
            ref.at[t], wqkv.at[i, :, pl.ds(t * local, local)], load_sem.at[11 + i * 3 + t]
        )
        for i, ref in ((1, col_qkv), (0, row_qkv))
        for t in range(3)
    ]
    own = [
        pltpu.make_async_copy(samples.at[:, chunk(k)], gathered.at[k, head], own_sem.at[k])
        for k in range(chunks)
    ]
    out_loads = []
    for j in range(4):
        for i, ref in enumerate((row_out, col_out)):
            out_loads.append(
                pltpu.make_async_copy(
                    ref.at[:, pl.ds(j * feat, feat)],
                    wout.at[j, pl.ds(i * local, local)],
                    load_sem.at[2 + j * 2 + i],
                )
            )
    gain_load = pltpu.make_async_copy(gain_hbm, gain, load_sem.at[10])
    own[0].start()
    for copy in [gain_load] + loads + own[1:] + out_loads:
        copy.start()

    barrier = pltpu.get_barrier_semaphore()
    pl.semaphore_signal(barrier, inc=1, device_id={"head": x_peer}, device_id_type=MESH)
    pl.semaphore_signal(barrier, inc=1, device_id={"head": core_peer}, device_id_type=MESH)
    for d in range(1, n):
        pl.semaphore_signal(barrier, inc=1, device_id={"row": lax.rem(me + d, n)}, device_id_type=MESH)
    pl.semaphore_wait(barrier, n + 1)

    def remote(src, dst, sems, where, peer):
        return pltpu.make_async_remote_copy(
            src_ref=src, dst_ref=dst, send_sem=sems.at[(0,) + where], recv_sem=sems.at[(1,) + where],
            device_id=peer, device_id_type=MESH,
        )

    x_copies = {
        (k, r): remote(
            samples.at[r, chunk(k)], gathered.at[k, head, r], x_sem, (k, r), {"head": x_peer}
        )
        for k in range(chunks)
        for r in range(rows)
    }
    core_copies = [
        remote(samples.at[:, chunk(k)], gathered.at[k, head], core_sem, (k,), {"head": core_peer})
        for k in range(chunks)
    ]
    fwd_copies = {
        (k, r): remote(
            gathered.at[k, x_peer, r], gathered.at[k, x_peer, r], fwd_sem, (k, r), {"head": core_peer}
        )
        for k in range(chunks)
        for r in range(rows)
    }
    col_copies, back_copies, part_copies, cross_copies, stores = {}, {}, {}, {}, {}

    def send_samples(k):
        if k < chunks:
            for r in range(rows):
                x_copies[k, r].start()
            core_copies[k].start()

    def pass_on(k):
        for r in range(rows):
            x_copies[k, r].wait_recv()
            fwd_copies[k, r].start()
        if k == 0:
            send_samples(1)
        send_samples(k + 2)

    def normalise(k, r):
        step, lane = 64, 128
        tiles = [(j, pl.ds(l * lane, lane), pl.ds(j * feat + l * lane, lane))
                 for j in range(4) for l in range(feat // lane)]
        for i in range(width // step):
            at = pl.ds(i * step, step)
            to = pl.ds(r * width + i * step, step)

            def tile(j, lanes):
                return gathered[k, j, r, at, lanes].astype(F32)

            total = sum(tile(j, lanes) for j, lanes, _ in tiles)
            mean = jnp.sum(total, axis=-1, keepdims=True) * (1.0 / (4 * feat))
            total = sum((tile(j, lanes) - mean) ** 2 for j, lanes, _ in tiles)
            var = jnp.sum(total, axis=-1, keepdims=True) * (1.0 / (4 * feat))
            inv = lax.rsqrt(var + 1e-05)
            for j, lanes, whole in tiles:
                normed[to, whole] = ((tile(j, lanes) - mean) * inv * gain[:, whole]).astype(BF16)

    def project(k):
        own[k].wait()
        core_copies[k].wait_recv()
        if k == 0:
            gain_load.wait()
        for r in range(rows):
            fwd_copies[k, r].wait_recv()
            normalise(k, r)

        if k == 0:
            for copy in loads:
                copy.wait()

        def mixed(group):
            value = jnp.dot(normed[...], wqkv[group], preferred_element_type=F32).astype(BF16)
            return [value[:, t * local:(t + 1) * local].reshape(rows, width, local) for t in range(3)]

        for t, value in enumerate(mixed(1)):
            col_send[k, t] = value

        for d in range(1, n):
            peer = lax.rem(me + d, n)
            cut = pl.ds(pl.multiple_of(peer * each, each), each)
            col_copies[k, d] = remote(
                col_send.at[k, :, :, cut], col_recv.at[k, me], col_sem, (k, d), {"row": peer}
            )
            col_copies[k, d].start()
        mine = pl.ds(pl.multiple_of(me * each, each), each)
        col_recv[k, me] = col_send[k, :, :, mine, :]

        for t, value in enumerate(mixed(0)):
            row_store[t, :, chunk(k), :] = value

    def row_attend(k):
        seen = (k + 1) * width
        i = lax.broadcasted_iota(jnp.int32, (width, seen), 0) + k * width
        j = lax.broadcasted_iota(jnp.int32, (width, seen), 1)
        for r in range(rows):
            for h in range(heads):
                lanes = pl.ds(h * HD, HD)
                row_attn[k, r, :, lanes] = attend(
                    row_store[0, r, chunk(k), lanes],
                    row_store[1, r, pl.ds(0, seen), lanes],
                    row_store[2, r, pl.ds(0, seen), lanes],
                    j <= i,
                )

    def col_attend(k):
        for d in range(1, n):
            col_copies[k, d].wait_recv()
        for first, last in ((0, n // 2), (n // 2, n)):
            held, asking = last * rows * each, (last - first) * rows * each
            i = lax.broadcasted_iota(jnp.int32, (asking, held), 0) + (held - asking)
            j = lax.broadcasted_iota(jnp.int32, (asking, held), 1)
            allowed = (j <= i) & (lax.rem(i, each) == lax.rem(j, each))
            for h in range(heads):
                lanes = pl.ds(h * HD, HD)
                query = col_recv[k, first:last, 0, :, :, lanes].reshape(asking, HD)
                parts = [col_recv[k, :last, t, :, :, lanes].reshape(held, HD) for t in (1, 2)]
                col_done[k, first:last, :, :, lanes] = attend(query, *parts, allowed).reshape(
                    last - first, rows, each, HD
                )
        mine = pl.ds(pl.multiple_of(me * each, each), each)
        for d in range(1, n):
            peer = lax.rem(me + d, n)
            back_copies[k, d] = remote(
                col_done.at[k, peer], col_back.at[k, :, mine], back_sem, (k, d), {"row": peer}
            )
            back_copies[k, d].start()
        col_back[k, :, mine, :] = col_done[k, me]

    def finish(k):
        if k == 0:
            for copy in out_loads:
                copy.wait()
        for d in range(1, n):
            back_copies[k, d].wait_recv()
        attn = jnp.concatenate(
            [row_attn[k].reshape(tokens, local), col_back[k].reshape(tokens, local)], axis=-1
        )

        def block(j):
            return jnp.dot(attn, wout[j], preferred_element_type=F32)

        for s, xb in enumerate((x_other, x_own)):
            part_send[k, s] = block(xb * 2 + core_other).astype(BF16).reshape(rows, width, feat)
            part_copies[k, s] = remote(
                part_send.at[k, s], part_recv.at[k, s], part_sem, (k, s), {"head": core_peer}
            )
            part_copies[k, s].start()
        for s, xb in enumerate((x_other, x_own)):
            kept[k, s] = block(xb * 2 + core).reshape(rows, width, feat)

    def cross(k):
        part_copies[k, 0].wait_recv()
        cross_send[k] = (kept[k, 0] + part_recv[k, 0].astype(F32)).astype(BF16)
        cross_copies[k] = remote(
            cross_send.at[k], cross_recv.at[k], cross_sem, (k,), {"head": x_peer}
        )
        cross_copies[k].start()

    def close(k):
        part_copies[k, 1].wait_recv()
        cross_copies[k].wait_recv()
        total = kept[k, 1] + part_recv[k, 1].astype(F32) + cross_recv[k].astype(F32)
        result[k] = (gathered[k, head].astype(F32) + total).astype(BF16)
        stores[k] = pltpu.make_async_copy(result.at[k], out.at[:, chunk(k)], store_sem.at[k])
        stores[k].start()

    send_samples(0)
    pass_on(0)
    project(0)
    pass_on(1)
    row_attend(0)
    project(1)
    pass_on(2)
    row_attend(1)
    project(2)
    col_attend(0)
    pass_on(3)
    row_attend(2)
    project(3)
    row_attend(3)
    col_attend(1)
    finish(0)
    cross(0)
    col_attend(2)
    finish(1)
    cross(1)
    close(0)
    col_attend(3)
    finish(2)
    cross(2)
    close(1)
    finish(3)
    cross(3)
    close(2)
    close(3)

    for copy in core_copies:
        copy.wait_send()
    for group in (x_copies, fwd_copies, col_copies, back_copies, part_copies, cross_copies):
        for copy in group.values():
            copy.wait_send()
    for copy in stores.values():
        copy.wait()


def fused(n, samples, norm_gain, row_qkv, col_qkv, row_out, col_out):
    rows, cols, feat = samples.shape
    chunks = 4
    width = cols // chunks
    each = width // n
    local = row_qkv.shape[2]
    dma = pltpu.SemaphoreType.DMA
    anywhere = pl.BlockSpec(memory_space=pl.ANY)
    return pl.pallas_call(
        functools.partial(layer_kernel, n, chunks),
        out_shape=jax.ShapeDtypeStruct(samples.shape, samples.dtype),
        in_specs=[anywhere] * 6,
        out_specs=anywhere,
        scratch_shapes=[
            pltpu.VMEM((1, 4 * feat), F32),
            pltpu.VMEM((chunks, 4, rows, width, feat), BF16),
            pltpu.VMEM((2, 4 * feat, 3 * local), BF16),
            pltpu.VMEM((4, 2 * local, feat), BF16),
            pltpu.VMEM((rows * width, 4 * feat), BF16),
            pltpu.VMEM((3, rows, cols, local), BF16),
            pltpu.VMEM((chunks, 3, rows, width, local), BF16),
            pltpu.VMEM((chunks, n, 3, rows, each, local), BF16),
            pltpu.VMEM((chunks, n, rows, each, local), BF16),
            pltpu.VMEM((chunks, rows, width, local), BF16),
            pltpu.VMEM((chunks, rows, width, local), BF16),
            pltpu.VMEM((chunks, 2, rows, width, feat), BF16),
            pltpu.VMEM((chunks, 2, rows, width, feat), BF16),
            pltpu.VMEM((chunks, 2, rows, width, feat), F32),
            pltpu.VMEM((chunks, rows, width, feat), BF16),
            pltpu.VMEM((chunks, rows, width, feat), BF16),
            pltpu.VMEM((chunks, rows, width, feat), BF16),
            dma((17,)),
            dma((chunks,)),
            dma((chunks,)),
            dma((2, chunks, rows)),
            dma((2, chunks)),
            dma((2, chunks, rows)),
            dma((2, chunks, n)),
            dma((2, chunks, n)),
            dma((2, chunks, 2)),
            dma((2, chunks)),
        ],
        compiler_params=pltpu.CompilerParams(
            collective_id=0, has_side_effects=True, vmem_limit_bytes=52 * 2**20
        ),
        cost_estimate=pl.CostEstimate(flops=9 * 10**9, bytes_accessed=11 * 2**20, transcendentals=10**6),
    )(samples, norm_gain.reshape(1, -1), row_qkv, col_qkv, row_out, col_out)


def layer_norm(values, norm_gain):
    values = values.astype(F32)
    mean = jnp.mean(values, axis=-1, keepdims=True)
    centred = values - mean
    var = jnp.mean(centred * centred, axis=-1, keepdims=True)
    return (centred * lax.rsqrt(var + 1e-05) * norm_gain).astype(BF16)


def softmax_rounded(scores, allowed):
    scores = jnp.where(allowed, scores, -jnp.inf)
    top = jnp.max(scores, axis=-1, keepdims=True)
    expo = jnp.exp(scores - top)
    return (expo / jnp.sum(expo, axis=-1, keepdims=True)).astype(BF16)


def column_attend(query, keys, vals):
    full_rows = query.shape[0]
    scores = jnp.einsum("qche,kche->chqk", query, keys, preferred_element_type=F32) * (1.0 / HD**0.5)
    allowed = jnp.arange(full_rows)[:, None] >= jnp.arange(full_rows)[None, :]
    weights = softmax_rounded(scores, allowed[None, None])
    return jnp.einsum("chqk,kche->qche", weights, vals, preferred_element_type=F32).astype(BF16)


def unfused(samples, norm_gain, row_qkv, col_qkv, row_out, col_out):
    rows_local, cols, feat_local = samples.shape
    tokens_local = rows_local * cols
    whole = lax.all_gather(samples, "head", axis=2, tiled=True)
    normed = layer_norm(whole, norm_gain).reshape(tokens_local, -1)

    def project(weights):
        mixed = jnp.einsum("nd,tde->tne", normed, weights, preferred_element_type=F32)
        return mixed.astype(BF16).reshape(3, rows_local, cols, -1, HD)

    stacked = project(row_qkv)
    scores = jnp.einsum("rqhe,rkhe->rhqk", stacked[0], stacked[1], preferred_element_type=F32)
    allowed = jnp.arange(cols)[:, None] >= jnp.arange(cols)[None, :]
    weights = softmax_rounded(scores * (1.0 / HD**0.5), allowed[None, None])
    attended = jnp.einsum("rhqk,rkhe->rqhe", weights, stacked[2], preferred_element_type=F32)
    row_attn = attended.astype(BF16).reshape(tokens_local, -1)
    moved = column_attend(
        *(lax.all_to_all(part, "row", split_axis=1, concat_axis=0, tiled=True) for part in project(col_qkv))
    )
    returned = lax.all_to_all(moved, "row", split_axis=0, concat_axis=1, tiled=True)
    partial_term = jnp.dot(row_attn, row_out, preferred_element_type=F32)
    partial_term = partial_term + jnp.dot(
        returned.reshape(tokens_local, -1), col_out, preferred_element_type=F32
    )
    summed = lax.psum_scatter(partial_term.astype(BF16), "head", scatter_dimension=1, tiled=True)
    total = samples.astype(F32) + summed.astype(F32).reshape(rows_local, cols, feat_local)
    return total.astype(BF16)


def solution(mesh):
    n = mesh.shape["row"]

    def shards(samples, *rest):
        if mesh.shape["head"] == 4 and samples.shape[1] % (4 * 16 * n) == 0:
            return fused(n, samples, *rest)
        return unfused(samples, *rest)

    placed = (
        P("row", None, "head"),
        P(),
        P(None, None, "head"),
        P(None, None, "head"),
        P("head", None),
        P("head", None),
    )
    return jax.shard_map(
        shards, mesh=mesh, in_specs=placed, out_specs=P("row", None, "head"), check_vma=False
    )
```

```python
import functools

import jax
import jax.numpy as jnp
from jax import lax
from jax.experimental import pallas as pl
from jax.experimental.pallas import tpu as pltpu
from jax.sharding import PartitionSpec as P

HD = 128
LOG2E = 1.4426950408889634
MESH = pl.DeviceIdType.MESH
F32 = jnp.float32
BF16 = jnp.bfloat16


def attend(query, keys, vals, allowed):
    scores = lax.dot_general(query, keys, (((1,), (1,)), ((), ())), preferred_element_type=F32)
    scores = jnp.where(allowed, scores, -jnp.inf)
    expo = jnp.exp2((scores - jnp.max(scores, axis=-1, keepdims=True)) * (LOG2E / HD**0.5))
    total = jnp.sum(expo, axis=-1, keepdims=True)
    out = jnp.dot(expo.astype(BF16), vals, preferred_element_type=F32)
    return (out / total).astype(BF16)


def layer_kernel(
    n, chunks,
    samples, gain_hbm, row_qkv, col_qkv, row_out, col_out, out,
    gain, gathered, wqkv, wout, normed, row_store, col_send, col_recv, col_done, col_back, row_attn,
    part_send, part_recv, kept, cross_send, cross_recv, result,
    load_sem, own_sem, store_sem, x_sem, core_sem, fwd_sem, col_sem, back_sem, part_sem, cross_sem,
):
    rows, cols, feat = samples.shape
    width = cols // chunks
    tokens = rows * width
    each = width // n
    local = row_qkv.shape[2]
    heads = local // HD
    me = lax.axis_index("row")
    head = lax.axis_index("head")
    x_own = head // 2
    core = head % 2
    x_other = 1 - x_own
    core_other = 1 - core
    x_peer = x_other * 2 + core
    core_peer = x_own * 2 + core_other

    def chunk(k):
        return pl.ds(k * width, width)

    loads = [
        pltpu.make_async_copy(
            ref.at[t], wqkv.at[i, :, pl.ds(t * local, local)], load_sem.at[11 + i * 3 + t]
        )
        for i, ref in ((1, col_qkv), (0, row_qkv))
        for t in range(3)
    ]
    own = [
        pltpu.make_async_copy(samples.at[:, chunk(k)], gathered.at[k, head], own_sem.at[k])
        for k in range(chunks)
    ]
    out_loads = []
    for j in range(4):
        for i, ref in enumerate((row_out, col_out)):
            out_loads.append(
                pltpu.make_async_copy(
                    ref.at[:, pl.ds(j * feat, feat)],
                    wout.at[j, pl.ds(i * local, local)],
                    load_sem.at[2 + j * 2 + i],
                )
            )
    gain_load = pltpu.make_async_copy(gain_hbm, gain, load_sem.at[10])
    own[0].start()
    for copy in [gain_load] + loads + own[1:] + out_loads:
        copy.start()

    barrier = pltpu.get_barrier_semaphore()
    pl.semaphore_signal(barrier, inc=1, device_id={"head": x_peer}, device_id_type=MESH)
    pl.semaphore_signal(barrier, inc=1, device_id={"head": core_peer}, device_id_type=MESH)
    for d in range(1, n):
        pl.semaphore_signal(barrier, inc=1, device_id={"row": lax.rem(me + d, n)}, device_id_type=MESH)
    pl.semaphore_wait(barrier, n + 1)

    def remote(src, dst, sems, where, peer):
        return pltpu.make_async_remote_copy(
            src_ref=src, dst_ref=dst, send_sem=sems.at[(0,) + where], recv_sem=sems.at[(1,) + where],
            device_id=peer, device_id_type=MESH,
        )

    x_copies = {
        (k, r): remote(
            samples.at[r, chunk(k)], gathered.at[k, head, r], x_sem, (k, r), {"head": x_peer}
        )
        for k in range(chunks)
        for r in range(rows)
    }
    core_copies = [
        remote(samples.at[:, chunk(k)], gathered.at[k, head], core_sem, (k,), {"head": core_peer})
        for k in range(chunks)
    ]
    fwd_copies = {
        (k, r): remote(
            gathered.at[k, x_peer, r], gathered.at[k, x_peer, r], fwd_sem, (k, r), {"head": core_peer}
        )
        for k in range(chunks)
        for r in range(rows)
    }
    col_copies, back_copies, part_copies, cross_copies, stores = {}, {}, {}, {}, {}

    def send_samples(k):
        if k < chunks:
            for r in range(rows):
                x_copies[k, r].start()
            core_copies[k].start()

    def pass_on(k):
        for r in range(rows):
            x_copies[k, r].wait_recv()
            fwd_copies[k, r].start()
        if k == 0:
            send_samples(1)
        send_samples(k + 2)

    def normalise(k, r):
        step, lane = 64, 128
        tiles = [(j, pl.ds(l * lane, lane), pl.ds(j * feat + l * lane, lane))
                 for j in range(4) for l in range(feat // lane)]
        for i in range(width // step):
            at = pl.ds(i * step, step)
            to = pl.ds(r * width + i * step, step)

            def tile(j, lanes):
                return gathered[k, j, r, at, lanes].astype(F32)

            total = sum(tile(j, lanes) for j, lanes, _ in tiles)
            mean = jnp.sum(total, axis=-1, keepdims=True) * (1.0 / (4 * feat))
            total = sum((tile(j, lanes) - mean) ** 2 for j, lanes, _ in tiles)
            var = jnp.sum(total, axis=-1, keepdims=True) * (1.0 / (4 * feat))
            inv = lax.rsqrt(var + 1e-05)
            for j, lanes, whole in tiles:
                normed[to, whole] = ((tile(j, lanes) - mean) * inv * gain[:, whole]).astype(BF16)

    def project(k):
        own[k].wait()
        core_copies[k].wait_recv()
        if k == 0:
            gain_load.wait()
        for r in range(rows):
            fwd_copies[k, r].wait_recv()
            normalise(k, r)

        if k == 0:
            for copy in loads:
                copy.wait()

        def mixed(group):
            value = jnp.dot(normed[...], wqkv[group], preferred_element_type=F32).astype(BF16)
            return [value[:, t * local:(t + 1) * local].reshape(rows, width, local) for t in range(3)]

        for t, value in enumerate(mixed(1)):
            col_send[k, t] = value

        for d in range(1, n):
            peer = lax.rem(me + d, n)
            cut = pl.ds(pl.multiple_of(peer * each, each), each)
            col_copies[k, d] = remote(
                col_send.at[k, :, :, cut], col_recv.at[k, me], col_sem, (k, d), {"row": peer}
            )
            col_copies[k, d].start()
        mine = pl.ds(pl.multiple_of(me * each, each), each)
        col_recv[k, me] = col_send[k, :, :, mine, :]

        for t, value in enumerate(mixed(0)):
            row_store[t, :, chunk(k), :] = value

    def row_attend(k):
        seen = (k + 1) * width
        i = lax.broadcasted_iota(jnp.int32, (width, seen), 0) + k * width
        j = lax.broadcasted_iota(jnp.int32, (width, seen), 1)
        for r in range(rows):
            for h in range(heads):
                lanes = pl.ds(h * HD, HD)
                row_attn[k, r, :, lanes] = attend(
                    row_store[0, r, chunk(k), lanes],
                    row_store[1, r, pl.ds(0, seen), lanes],
                    row_store[2, r, pl.ds(0, seen), lanes],
                    j <= i,
                )

    def col_attend(k):
        for d in range(1, n):
            col_copies[k, d].wait_recv()
        for first, last in ((0, n // 2), (n // 2, n)):
            held, asking = last * rows * each, (last - first) * rows * each
            i = lax.broadcasted_iota(jnp.int32, (asking, held), 0) + (held - asking)
            j = lax.broadcasted_iota(jnp.int32, (asking, held), 1)
            allowed = (j <= i) & (lax.rem(i, each) == lax.rem(j, each))
            for h in range(heads):
                lanes = pl.ds(h * HD, HD)
                query = col_recv[k, first:last, 0, :, :, lanes].reshape(asking, HD)
                parts = [col_recv[k, :last, t, :, :, lanes].reshape(held, HD) for t in (1, 2)]
                col_done[k, first:last, :, :, lanes] = attend(query, *parts, allowed).reshape(
                    last - first, rows, each, HD
                )
        mine = pl.ds(pl.multiple_of(me * each, each), each)
        for d in range(1, n):
            peer = lax.rem(me + d, n)
            back_copies[k, d] = remote(
                col_done.at[k, peer], col_back.at[k, :, mine], back_sem, (k, d), {"row": peer}
            )
            back_copies[k, d].start()
        col_back[k, :, mine, :] = col_done[k, me]

    def finish(k):
        if k == 0:
            for copy in out_loads:
                copy.wait()
        for d in range(1, n):
            back_copies[k, d].wait_recv()
        attn = jnp.concatenate(
            [row_attn[k].reshape(tokens, local), col_back[k].reshape(tokens, local)], axis=-1
        )

        def block(j):
            return jnp.dot(attn, wout[j], preferred_element_type=F32)

        for s, xb in enumerate((x_other, x_own)):
            part_send[k, s] = block(xb * 2 + core_other).astype(BF16).reshape(rows, width, feat)
            part_copies[k, s] = remote(
                part_send.at[k, s], part_recv.at[k, s], part_sem, (k, s), {"head": core_peer}
            )
            part_copies[k, s].start()
        for s, xb in enumerate((x_other, x_own)):
            kept[k, s] = block(xb * 2 + core).reshape(rows, width, feat)

    def cross(k):
        part_copies[k, 0].wait_recv()
        cross_send[k] = (kept[k, 0] + part_recv[k, 0].astype(F32)).astype(BF16)
        cross_copies[k] = remote(
            cross_send.at[k], cross_recv.at[k], cross_sem, (k,), {"head": x_peer}
        )
        cross_copies[k].start()

    def close(k):
        part_copies[k, 1].wait_recv()
        cross_copies[k].wait_recv()
        total = kept[k, 1] + part_recv[k, 1].astype(F32) + cross_recv[k].astype(F32)
        result[k] = (gathered[k, head].astype(F32) + total).astype(BF16)
        stores[k] = pltpu.make_async_copy(result.at[k], out.at[:, chunk(k)], store_sem.at[k])
        stores[k].start()

    send_samples(0)
    pass_on(0)
    project(0)
    pass_on(1)
    row_attend(0)
    project(1)
    pass_on(2)
    row_attend(1)
    project(2)
    col_attend(0)
    pass_on(3)
    row_attend(2)
    finish(0)
    project(3)
    cross(0)
    col_attend(1)
    row_attend(3)
    finish(1)
    col_attend(2)
    cross(1)
    close(0)
    finish(2)
    col_attend(3)
    cross(2)
    close(1)
    finish(3)
    cross(3)
    close(2)
    close(3)

    for copy in core_copies:
        copy.wait_send()
    for group in (x_copies, fwd_copies, col_copies, back_copies, part_copies, cross_copies):
        for copy in group.values():
            copy.wait_send()
    for copy in stores.values():
        copy.wait()


def fused(n, samples, norm_gain, row_qkv, col_qkv, row_out, col_out):
    rows, cols, feat = samples.shape
    chunks = 4
    width = cols // chunks
    each = width // n
    local = row_qkv.shape[2]
    dma = pltpu.SemaphoreType.DMA
    anywhere = pl.BlockSpec(memory_space=pl.ANY)
    return pl.pallas_call(
        functools.partial(layer_kernel, n, chunks),
        out_shape=jax.ShapeDtypeStruct(samples.shape, samples.dtype),
        in_specs=[anywhere] * 6,
        out_specs=anywhere,
        scratch_shapes=[
            pltpu.VMEM((1, 4 * feat), F32),
            pltpu.VMEM((chunks, 4, rows, width, feat), BF16),
            pltpu.VMEM((2, 4 * feat, 3 * local), BF16),
            pltpu.VMEM((4, 2 * local, feat), BF16),
            pltpu.VMEM((rows * width, 4 * feat), BF16),
            pltpu.VMEM((3, rows, cols, local), BF16),
            pltpu.VMEM((chunks, 3, rows, width, local), BF16),
            pltpu.VMEM((chunks, n, 3, rows, each, local), BF16),
            pltpu.VMEM((chunks, n, rows, each, local), BF16),
            pltpu.VMEM((chunks, rows, width, local), BF16),
            pltpu.VMEM((chunks, rows, width, local), BF16),
            pltpu.VMEM((chunks, 2, rows, width, feat), BF16),
            pltpu.VMEM((chunks, 2, rows, width, feat), BF16),
            pltpu.VMEM((chunks, 2, rows, width, feat), F32),
            pltpu.VMEM((chunks, rows, width, feat), BF16),
            pltpu.VMEM((chunks, rows, width, feat), BF16),
            pltpu.VMEM((chunks, rows, width, feat), BF16),
            dma((17,)),
            dma((chunks,)),
            dma((chunks,)),
            dma((2, chunks, rows)),
            dma((2, chunks)),
            dma((2, chunks, rows)),
            dma((2, chunks, n)),
            dma((2, chunks, n)),
            dma((2, chunks, 2)),
            dma((2, chunks)),
        ],
        compiler_params=pltpu.CompilerParams(
            collective_id=0, has_side_effects=True, vmem_limit_bytes=52 * 2**20
        ),
        cost_estimate=pl.CostEstimate(flops=9 * 10**9, bytes_accessed=11 * 2**20, transcendentals=10**6),
    )(samples, norm_gain.reshape(1, -1), row_qkv, col_qkv, row_out, col_out)


def layer_norm(values, norm_gain):
    values = values.astype(F32)
    mean = jnp.mean(values, axis=-1, keepdims=True)
    centred = values - mean
    var = jnp.mean(centred * centred, axis=-1, keepdims=True)
    return (centred * lax.rsqrt(var + 1e-05) * norm_gain).astype(BF16)


def softmax_rounded(scores, allowed):
    scores = jnp.where(allowed, scores, -jnp.inf)
    top = jnp.max(scores, axis=-1, keepdims=True)
    expo = jnp.exp(scores - top)
    return (expo / jnp.sum(expo, axis=-1, keepdims=True)).astype(BF16)


def column_attend(query, keys, vals):
    full_rows = query.shape[0]
    scores = jnp.einsum("qche,kche->chqk", query, keys, preferred_element_type=F32) * (1.0 / HD**0.5)
    allowed = jnp.arange(full_rows)[:, None] >= jnp.arange(full_rows)[None, :]
    weights = softmax_rounded(scores, allowed[None, None])
    return jnp.einsum("chqk,kche->qche", weights, vals, preferred_element_type=F32).astype(BF16)


def unfused(samples, norm_gain, row_qkv, col_qkv, row_out, col_out):
    rows_local, cols, feat_local = samples.shape
    tokens_local = rows_local * cols
    whole = lax.all_gather(samples, "head", axis=2, tiled=True)
    normed = layer_norm(whole, norm_gain).reshape(tokens_local, -1)

    def project(weights):
        mixed = jnp.einsum("nd,tde->tne", normed, weights, preferred_element_type=F32)
        return mixed.astype(BF16).reshape(3, rows_local, cols, -1, HD)

    stacked = project(row_qkv)
    scores = jnp.einsum("rqhe,rkhe->rhqk", stacked[0], stacked[1], preferred_element_type=F32)
    allowed = jnp.arange(cols)[:, None] >= jnp.arange(cols)[None, :]
    weights = softmax_rounded(scores * (1.0 / HD**0.5), allowed[None, None])
    attended = jnp.einsum("rhqk,rkhe->rqhe", weights, stacked[2], preferred_element_type=F32)
    row_attn = attended.astype(BF16).reshape(tokens_local, -1)
    moved = column_attend(
        *(lax.all_to_all(part, "row", split_axis=1, concat_axis=0, tiled=True) for part in project(col_qkv))
    )
    returned = lax.all_to_all(moved, "row", split_axis=0, concat_axis=1, tiled=True)
    partial_term = jnp.dot(row_attn, row_out, preferred_element_type=F32)
    partial_term = partial_term + jnp.dot(
        returned.reshape(tokens_local, -1), col_out, preferred_element_type=F32
    )
    summed = lax.psum_scatter(partial_term.astype(BF16), "head", scatter_dimension=1, tiled=True)
    total = samples.astype(F32) + summed.astype(F32).reshape(rows_local, cols, feat_local)
    return total.astype(BF16)


def solution(mesh):
    n = mesh.shape["row"]

    def shards(samples, *rest):
        if mesh.shape["head"] == 4 and samples.shape[1] % (4 * 16 * n) == 0:
            return fused(n, samples, *rest)
        return unfused(samples, *rest)

    placed = (
        P("row", None, "head"),
        P(),
        P(None, None, "head"),
        P(None, None, "head"),
        P("head", None),
        P("head", None),
    )
    return jax.shard_map(
        shards, mesh=mesh, in_specs=placed, out_specs=P("row", None, "head"), check_vma=False
    )
```
